512 devices in a mesh: phase: 32 (over y, x), tp: 8 (over z_lo, core), dp: 2 (over z_hi).
Axes of the slice: x: 4, y: 8, z: 8 (z_hi: 2, z_lo: 4; z = z_hi * 4 + z_lo), core: 2. Of those that a mesh axis runs over, the one named last changes fastest.
Arguments:
- down_inputs: bfloat16 [2, 32, 128, 1280], P('dp', 'phase', None, 'tp'), may hold values from -6 to 6
- up_inputs: bfloat16 [2, 32, 128, 1280], P('dp', 'phase', None, 'tp'), may hold values from -6 to 6
- down_cot: bfloat16 [2, 32, 128, 1280], P('dp', 'phase', None, 'tp'), may hold values from -6 to 6
- up_cot: bfloat16 [2, 32, 128, 1280], P('dp', 'phase', None, 'tp'), may hold values from -6 to 6
- segment_ids: int32 [2, 2, 32, 128], P(None, 'dp'), may hold values from 0 to 3, never falling along the last dimension, each value on 1 to 64 neighbouring positions
- patch_rows: int32 [2, 2, 32, 128], P(None, 'dp'), may hold values from 0 to 31
- patch_cols: int32 [2, 2, 32, 128], P(None, 'dp'), may hold values from 0 to 31
- w_qkv: bfloat16 [32, 3, 1280, 1280], P('phase', None, 'tp'), may hold values from -0.15625 to 0.15625
- w_out: bfloat16 [32, 1280, 1280], P('phase', 'tp'), may hold values from -0.15625 to 0.15625
Outputs:
- down_input_grad: bfloat16 [2, 32, 128, 1280], P('dp', 'phase', None, 'tp')
- up_input_grad: bfloat16 [2, 32, 128, 1280], P('dp', 'phase', None, 'tp')
- grad_qkv: bfloat16 [32, 3, 1280, 1280], P('phase', None, 'tp')
- grad_out: bfloat16 [32, 1280, 1280], P('phase', 'tp')
The draws below stay inside these ranges and needn't reach their ends.
All inputs are finite; a program needn't handle non-finite values.
Results may differ from the reference program's by a relative error of at most 0.023.
Values may be sent and summed in bfloat16 or wider, within the bound.
A program may use at most 64 MiB of HBM per device.

```python
import math
import jax
import jax.numpy as jnp
import numpy as np
from jax import lax

D = 1280
HEADS = 16
HD = 80
TOK = 128
PHASES = 32
REPLICAS = 2


def touch_ends(drawn, stream_key, low, top_value):
    index_at = [jax.random.randint(jax.random.fold_in(stream_key, axis), (), 0, length) for axis, length in enumerate(drawn.shape)]
    longest = drawn.shape.index(max(drawn.shape))
    beside = index_at[:longest] + [(index_at[longest] + 1) % drawn.shape[longest]] + index_at[longest + 1:]
    return drawn.at[tuple(index_at)].set(low).at[tuple(beside)].set(top_value)


def level_of(key, shape, shards, low, top_value):
    level, own = 1.0, jax.random.fold_in(key, 6)
    for dim, blocks in shards:
        steps = jnp.exp(jax.random.uniform(jax.random.fold_in(own, dim), (blocks,), jnp.float32, low / len(shards), top_value / len(shards)))
        level = level * jnp.repeat(steps, shape[dim] // blocks).reshape([-1 if axis == dim else 1 for axis in range(len(shape))])
    return level


def profile(count, total, most, skew):
    loads = [(1 << 20) // math.isqrt(grade ** skew) + 1 for grade in range(2, count + 1)]
    rest, given = total - most - (count - 1), [1] * (count - 1)
    while rest > 0:
        free = [i for i in range(count - 1) if given[i] < most]
        mass, left = sum([loads[i] for i in free]), rest
        for i in free:
            extra = min(most - given[i], max(1, left * loads[i] // mass), rest)
            given[i] = given[i] + extra
            rest = rest - extra
    return np.array([most] + given)


def uneven_parts(key, count, total, bound, skew):
    if count == 2:
        one = jax.random.randint(key, (), max(1, total - bound), min(bound, total - 1) + 1)
        return jnp.stack([one, total - one])
    lengths = jnp.asarray(profile(count, total, bound, skew), jnp.int32)
    pairs = (count - 1) // 2
    giver, sink = lengths[1:1 + 2 * pairs:2], lengths[2:2 + 2 * pairs:2]
    room = jnp.minimum(giver - 1, bound - sink)
    passed = jax.random.randint(jax.random.fold_in(key, 1), (pairs,), 0, 1 << 20) % (room + 1)
    lengths = lengths.at[1:1 + 2 * pairs:2].set(giver - passed).at[2:2 + 2 * pairs:2].set(sink + passed)
    return lengths[jax.random.permutation(jax.random.fold_in(key, 2), count)]


def bell_draw(key, shape, scale, bound, split=(), kind=jnp.bfloat16):
    level = level_of(key, shape, split, -0.22, 0.18) if split else 1.0
    entries = jax.random.normal(key, shape, jnp.float32) * scale * level
    return jnp.minimum(jnp.maximum(entries, -bound), bound).astype(kind)


def setup_inputs(seed: int = 0) -> dict:
    key_of = jax.random.split(jax.random.key(seed), 10)
    down_inputs = bell_draw(key_of[0], (REPLICAS, PHASES, TOK, D), 1.0, 6.0, ((0, 2), (1, 32), (3, 8)))
    up_inputs = bell_draw(key_of[1], (REPLICAS, PHASES, TOK, D), 1.0, 6.0, ((0, 2), (1, 32), (3, 8)))
    down_cot = bell_draw(key_of[2], (REPLICAS, PHASES, TOK, D), 1.0, 6.0, ((0, 2), (1, 32), (3, 8)))
    up_cot = bell_draw(key_of[3], (REPLICAS, PHASES, TOK, D), 1.0, 6.0, ((0, 2), (1, 32), (3, 8)))
    segment_ids = jax.vmap(lambda own: jnp.searchsorted(jnp.cumsum(uneven_parts(own, max(TOK // 32, 4), TOK, TOK // 2, 2)), jnp.arange(TOK), side="right"))(jax.random.split(key_of[4], 2 * REPLICAS * PHASES)).reshape((2, REPLICAS, PHASES, TOK)).astype(jnp.int32)
    patch_rows = touch_ends(jax.random.randint(key_of[5], (2, REPLICAS, PHASES, TOK), 0, 32), jax.random.fold_in(key_of[5], 1), 0, 31).astype(jnp.int32)
    patch_cols = touch_ends(jax.random.randint(key_of[6], (2, REPLICAS, PHASES, TOK), 0, 32), jax.random.fold_in(key_of[6], 1), 0, 31).astype(jnp.int32)
    w_qkv = bell_draw(key_of[7], (PHASES, 3, HEADS * HD, D), D ** -0.5, 0.15625, ((0, 32), (2, 8)))
    w_out = bell_draw(key_of[8], (PHASES, HEADS * HD, D), (HEADS * HD) ** -0.5, 0.15625, ((0, 32), (1, 8)))
    return {"down_inputs": down_inputs, "up_inputs": up_inputs, "down_cot": down_cot, "up_cot": up_cot, "segment_ids": segment_ids, "patch_rows": patch_rows, "patch_cols": patch_cols, "w_qkv": w_qkv, "w_out": w_out}


def normalize(vectors):
    average = lax.optimization_barrier(jnp.mean(vectors, axis=1, keepdims=True))
    centred = vectors - average
    spread = lax.optimization_barrier(jnp.mean(centred * centred, axis=1, keepdims=True))
    return centred * lax.rsqrt(spread + 1e-06)

def rotate(vectors, patch_row, patch_col):
    quarter = vectors.shape[1] // 4
    frequency = 10000.0 ** (-jnp.arange(quarter, dtype=jnp.float32) / quarter)

    def turn_pair(section, position):
        angles = position.astype(jnp.float32)[:, None] * frequency[None, :]
        cosine = jnp.cos(angles)
        sine_part = jnp.sin(angles)
        left = section[:, :quarter]
        right = section[:, quarter:]
        return jnp.concatenate([left * cosine - right * sine_part, left * sine_part + right * cosine], axis=1)
    return jnp.concatenate([turn_pair(vectors[:, :2 * quarter], patch_row), turn_pair(vectors[:, 2 * quarter:], patch_col)], axis=1)

def attend(query_raw, key_raw, value_raw, segments, patch_row, patch_col):
    queries = rotate(normalize(query_raw), patch_row, patch_col)
    key_rows = rotate(normalize(key_raw), patch_row, patch_col)
    scores = jnp.dot(queries, key_rows.T, precision=lax.Precision.HIGHEST) / math.sqrt(query_raw.shape[1])
    same_segment = segments[:, None] == segments[None, :]
    raised = jnp.where(same_segment, jnp.exp(scores), jnp.zeros_like(scores))
    weights_soft = raised / lax.optimization_barrier(jnp.sum(raised, axis=1, keepdims=True))
    return jnp.dot(weights_soft, value_raw, precision=lax.Precision.HIGHEST)

def attend_all(project, segments, patch_row, patch_col):
    row_count = project.shape[0]
    sections = project.reshape(row_count, 3, project.shape[1] // (3 * HD), HD)

    def one_head(query_raw, key_raw, value_raw):
        return attend(query_raw, key_raw, value_raw, segments, patch_row, patch_col)
    blended = jax.vmap(one_head, in_axes=1, out_axes=1)(sections[:, 0], sections[:, 1], sections[:, 2])
    return blended.reshape(row_count, -1)

def forward(inputs, w_project, w_output, segments, patch_row, patch_col):
    model_width = inputs.shape[1]
    flat_weight = w_project.reshape(-1, model_width)
    project = jnp.dot(inputs, flat_weight.T, preferred_element_type=jnp.float32)
    heads = attend_all(project, segments, patch_row, patch_col).astype(jnp.bfloat16)
    outputs = (inputs.astype(jnp.float32) + jnp.dot(heads, w_output, preferred_element_type=jnp.float32)).astype(jnp.bfloat16)
    return (outputs, project, heads)

def backward(grad_in, inputs, w_project, w_output, project, heads, segments, patch_row, patch_col):
    model_width = inputs.shape[1]
    flat_weight = w_project.reshape(-1, model_width)
    grad_output = jnp.dot(heads.T, grad_in, preferred_element_type=jnp.float32)
    grad_heads = jnp.dot(grad_in, w_output.T, preferred_element_type=jnp.float32)

    def core(values_in):
        return attend_all(values_in, segments, patch_row, patch_col)
    _, pullback = jax.vjp(core, project)
    grad_project = pullback(grad_heads)[0].astype(jnp.bfloat16)
    grad_weights = jnp.dot(grad_project.T, inputs, preferred_element_type=jnp.float32).reshape(w_project.shape)
    grad_inputs = (grad_in.astype(jnp.float32) + jnp.dot(grad_project, flat_weight, preferred_element_type=jnp.float32)).astype(jnp.bfloat16)
    return (grad_inputs, grad_weights, grad_output)

def from_below(stack):
    return jnp.concatenate([jnp.zeros_like(stack[:1]), stack[:-1]], axis=0)

def from_above(stack):
    return jnp.concatenate([stack[1:], jnp.zeros_like(stack[-1:])], axis=0)

def table_below(table):
    return jnp.concatenate([table[:1], table[:-1]], axis=0)

def table_above(table):
    return jnp.concatenate([table[1:], table[-1:]], axis=0)

def run_forward(args):
    return forward(*args)

def run_backward(args):
    return backward(*args)

def run_replica(down_x, up_x, down_g, up_g, segments, patch_row, patch_col, w_qkv, w_out):
    mirror_q = w_qkv[::-1]
    mirror_o = w_out[::-1]
    down_meta = (segments[0], patch_row[0], patch_col[0])
    up_meta = (segments[1], patch_row[1], patch_col[1])
    down_meta2 = tuple((table_below(table) for table in down_meta))
    up_meta2 = tuple((table_above(table) for table in up_meta))
    down_out1, down_proj1, down_head1 = lax.map(run_forward, (down_x, w_qkv, w_out) + down_meta)
    down_in2 = from_below(down_out1)
    _, down_proj2, down_head2 = lax.map(run_forward, (down_in2, w_qkv, w_out) + down_meta2)
    up_out1, up_proj1, up_head1 = lax.map(run_forward, (up_x, mirror_q, mirror_o) + up_meta)
    up_in2 = from_above(up_out1)
    _, up_proj2, up_head2 = lax.map(run_forward, (up_in2, mirror_q, mirror_o) + up_meta2)
    down_dx2, down_gq2, down_go2 = lax.map(run_backward, (down_g, down_in2, w_qkv, w_out, down_proj2, down_head2) + down_meta2)
    down_dx1, down_gq1, down_go1 = lax.map(run_backward, (from_above(down_dx2), down_x, w_qkv, w_out, down_proj1, down_head1) + down_meta)
    up_dx2, up_gq2, up_go2 = lax.map(run_backward, (up_g, up_in2, mirror_q, mirror_o, up_proj2, up_head2) + up_meta2)
    up_dx1, up_gq1, up_go1 = lax.map(run_backward, (from_below(up_dx2), up_x, mirror_q, mirror_o, up_proj1, up_head1) + up_meta)
    rounded_q = lax.optimization_barrier((up_gq1 + up_gq2).astype(jnp.bfloat16)).astype(jnp.float32)
    rounded_o = lax.optimization_barrier((up_go1 + up_go2).astype(jnp.bfloat16)).astype(jnp.float32)
    grads_q = down_gq1 + down_gq2 + rounded_q[::-1]
    grads_o = down_go1 + down_go2 + rounded_o[::-1]
    return (down_dx1, up_dx1, grads_q, grads_o)

def reference(down_inputs, up_inputs, down_cot, up_cot, segment_ids, patch_rows, patch_cols, w_qkv, w_out):
    down_list = []
    up_list = []
    grad_qkv = jnp.zeros(w_qkv.shape, jnp.float32)
    grad_out = jnp.zeros(w_out.shape, jnp.float32)
    for replica in range(REPLICAS):
        down_dx, up_dx, grads_q, grads_o = run_replica(down_inputs[replica], up_inputs[replica], down_cot[replica], up_cot[replica], segment_ids[:, replica], patch_rows[:, replica], patch_cols[:, replica], w_qkv, w_out)
        down_list.append(down_dx)
        up_list.append(up_dx)
        grad_qkv = grad_qkv + grads_q
        grad_out = grad_out + grads_o
    return (jnp.stack(down_list, axis=0), jnp.stack(up_list, axis=0), grad_qkv.astype(jnp.bfloat16), grad_out.astype(jnp.bfloat16))
```

```python
import math

import jax
import jax.numpy as jnp
from jax import lax
from jax.sharding import PartitionSpec as P

HD = 80


def from_behind(x, axis, by):
    length = lax.axis_size(axis)
    pairs = [(i, i + by) for i in range(length) if 0 <= i + by < length]
    return lax.ppermute(x, axis, pairs)


def normalize(vectors):
    average = jnp.mean(vectors, axis=1, keepdims=True)
    centred = vectors - average
    spread = jnp.mean(centred * centred, axis=1, keepdims=True)
    return centred * lax.rsqrt(spread + 1e-06)


def rotate(vectors, patch_row, patch_col):
    quarter = vectors.shape[1] // 4
    frequency = 10000.0 ** (-jnp.arange(quarter, dtype=jnp.float32) / quarter)

    def turn_pair(section, position):
        angles = position.astype(jnp.float32)[:, None] * frequency[None, :]
        cosine = jnp.cos(angles)
        sine_part = jnp.sin(angles)
        left = section[:, :quarter]
        right = section[:, quarter:]
        return jnp.concatenate(
            [left * cosine - right * sine_part, left * sine_part + right * cosine], axis=1
        )

    return jnp.concatenate(
        [
            turn_pair(vectors[:, : 2 * quarter], patch_row),
            turn_pair(vectors[:, 2 * quarter :], patch_col),
        ],
        axis=1,
    )


def attend(query_raw, key_raw, value_raw, segments, patch_row, patch_col):
    queries = rotate(normalize(query_raw), patch_row, patch_col)
    key_rows = rotate(normalize(key_raw), patch_row, patch_col)
    scores = jnp.dot(queries, key_rows.T, precision=lax.Precision.HIGHEST) / math.sqrt(
        query_raw.shape[1]
    )
    same_segment = segments[:, None] == segments[None, :]
    raised = jnp.where(same_segment, jnp.exp(scores), jnp.zeros_like(scores))
    weights_soft = raised / jnp.sum(raised, axis=1, keepdims=True)
    return jnp.dot(weights_soft, value_raw, precision=lax.Precision.HIGHEST)


def attend_all(project, segments, patch_row, patch_col):
    row_count = project.shape[0]
    sections = project.reshape(row_count, 3, project.shape[1] // (3 * HD), HD)

    def one_head(query_raw, key_raw, value_raw):
        return attend(query_raw, key_raw, value_raw, segments, patch_row, patch_col)

    blended = jax.vmap(one_head, in_axes=1, out_axes=1)(
        sections[:, 0], sections[:, 1], sections[:, 2]
    )
    return blended.reshape(row_count, -1)


def pull_heads(project, grad_heads, segments, patch_row, patch_col):

    def core(values_in):
        return attend_all(values_in, segments, patch_row, patch_col)

    _, pullback = jax.vjp(core, project)
    return pullback(grad_heads)[0]


def select_row(table, index):
    return lax.dynamic_index_in_dim(table, index, 0, keepdims=False)


def forward_layer(inputs, w_project, w_output, metadata, want_outputs):
    full = lax.all_gather(inputs, "tp", axis=2, tiled=True)
    flat_weight = w_project.reshape(-1, w_project.shape[2])
    project = jnp.einsum("brd,cd->brc", full, flat_weight, preferred_element_type=jnp.float32)
    heads = jax.vmap(attend_all)(project, *metadata).astype(jnp.bfloat16)
    outputs = None
    if want_outputs:
        term = jnp.einsum("brh,hd->brd", heads, w_output, preferred_element_type=jnp.float32)
        summed = lax.psum_scatter(
            term.astype(jnp.bfloat16), "tp", scatter_dimension=2, tiled=True
        )
        outputs = (inputs.astype(jnp.float32) + summed.astype(jnp.float32)).astype(jnp.bfloat16)
    return outputs, (full, project, heads)


def backward_layer(grads_in, w_project, w_output, metadata, stored):
    full, project, heads = stored
    grads_full = lax.all_gather(grads_in, "tp", axis=2, tiled=True)
    grad_output = jnp.einsum("brh,brd->hd", heads, grads_full, preferred_element_type=jnp.float32)
    grad_heads = jnp.einsum("brd,hd->brh", grads_full, w_output, preferred_element_type=jnp.float32)
    grad_project = jax.vmap(pull_heads)(project, grad_heads, *metadata).astype(jnp.bfloat16)
    flat_weight = w_project.reshape(-1, w_project.shape[2])
    grad_weight = jnp.einsum("brc,brd->cd", grad_project, full, preferred_element_type=jnp.float32)
    term = jnp.einsum("brc,cd->brd", grad_project, flat_weight, preferred_element_type=jnp.float32)
    summed = lax.psum_scatter(term.astype(jnp.bfloat16), "tp", scatter_dimension=2, tiled=True)
    grad_inputs = (grads_in.astype(jnp.float32) + summed.astype(jnp.float32)).astype(jnp.bfloat16)
    return grad_inputs, grad_weight, grad_output


def mirror(x):
    count = lax.axis_size("phase")
    return lax.ppermute(x, "phase", [(i, count - 1 - i) for i in range(count)])


def per_device(
    down_inputs, up_inputs, down_cot, up_cot, segment_ids, patch_rows, patch_cols, w_qkv, w_out
):
    phases = lax.axis_size("phase")
    position = lax.axis_index("phase")
    mirrored = mirror(jnp.stack([up_inputs[0, 0], up_cot[0, 0]]))
    first_in = jnp.stack([down_inputs[0, 0], mirrored[0]])
    last_cot = jnp.stack([down_cot[0, 0], mirrored[1]])
    w_project, w_output = w_qkv[0], w_out[0]

    def describe(index):
        other = phases - 1 - index
        return tuple(
            jnp.stack([select_row(table[0, 0], index), select_row(table[1, 0], other)])
            for table in (segment_ids, patch_rows, patch_cols)
        )

    first_meta = describe(position)
    second_meta = describe(jnp.maximum(position - 1, 0))
    first_out, first_stored = forward_layer(first_in, w_project, w_output, first_meta, True)
    second_in = from_behind(first_out, "phase", 1)
    _, second_stored = forward_layer(second_in, w_project, w_output, second_meta, False)
    second_dx, second_gq, second_go = backward_layer(
        last_cot, w_project, w_output, second_meta, second_stored
    )
    first_grads = from_behind(second_dx, "phase", -1)
    first_dx, first_gq, first_go = backward_layer(
        first_grads, w_project, w_output, first_meta, first_stored
    )
    total = jnp.concatenate([first_gq + second_gq, first_go + second_go]).astype(jnp.bfloat16)
    other = lax.ppermute(total, "dp", [(0, 1), (1, 0)])
    both = (total.astype(jnp.float32) + other.astype(jnp.float32)).astype(jnp.bfloat16)
    rows = w_project.shape[0] * w_project.shape[1]
    return (
        first_dx[0][None, None],
        mirror(first_dx[1])[None, None],
        both[:rows].reshape(w_qkv.shape),
        both[rows:].reshape(w_out.shape),
    )


def solution(mesh):
    return jax.shard_map(
        per_device,
        mesh=mesh,
        in_specs=(
            P("dp", "phase", None, "tp"),
            P("dp", "phase", None, "tp"),
            P("dp", "phase", None, "tp"),
            P("dp", "phase", None, "tp"),
            P(None, "dp", None, None),
            P(None, "dp", None, None),
            P(None, "dp", None, None),
            P("phase", None, "tp", None),
            P("phase", "tp", None),
        ),
        out_specs=(
            P("dp", "phase", None, "tp"),
            P("dp", "phase", None, "tp"),
            P("phase", None, "tp", None),
            P("phase", "tp", None),
        ),
        check_vma=False,
    )
```

```python
import functools
import math

import jax
import jax.numpy as jnp
from jax import lax
from jax.experimental import pallas as pl
from jax.experimental.pallas import tpu as pltpu
from jax.sharding import PartitionSpec as P

HD = 80
QUARTER = 20
TOK = 128
D = 1280
SHARD = 160
CHUNK = 320
CHIPS = 4
HEADS = 4
PHASES = 32
ROWS = 480
MESH = pl.DeviceIdType.MESH
F32 = jnp.float32
BF16 = jnp.bfloat16


def dot_nn(a, b):
    return lax.dot_general(a, b, (((1,), (0,)), ((), ())), preferred_element_type=F32)


def dot_nt(a, b):
    return lax.dot_general(a, b, (((1,), (1,)), ((), ())), preferred_element_type=F32)


def dot_tn(a, b):
    return lax.dot_general(a, b, (((0,), (0,)), ((), ())), preferred_element_type=F32)


def normalize(x):
    centred = x - jnp.mean(x, axis=0, keepdims=True)
    scale = lax.rsqrt(jnp.mean(centred * centred, axis=0, keepdims=True) + 1e-06)
    return centred * scale, scale


def pull_normalize(grad, y, scale):
    return scale * (
        grad
        - jnp.mean(grad, axis=0, keepdims=True)
        - y * jnp.mean(grad * y, axis=0, keepdims=True)
    )


def swap_pairs(y):
    row = lax.broadcasted_iota(jnp.int32, y.shape, 0)
    first = (row < QUARTER) | ((row >= 2 * QUARTER) & (row < 3 * QUARTER))
    return jnp.where(first, pltpu.roll(y, HD - QUARTER, axis=0), pltpu.roll(y, QUARTER, axis=0))


def identity(size):
    row = lax.broadcasted_iota(jnp.int32, (size, size), 0)
    column = lax.broadcasted_iota(jnp.int32, (size, size), 1)
    return jnp.where(row == column, 1.0, 0.0).astype(BF16)


def kernel(
    down_x,
    up_x,
    down_cot,
    up_cot,
    segments,
    patch_rows,
    patch_cols,
    w_qkv,
    w_out,
    out_down,
    out_up,
    out_qkv,
    out_wo,
    staged,
    meta,
    cosine,
    sine,
    mask,
    wq,
    wo,
    wq_t,
    wo_t,
    x1,
    x2,
    g1,
    g2,
    project,
    grad_o,
    ys,
    scales,
    qkv,
    weights,
    heads1,
    heads2,
    dp1,
    dp2,
    partial,
    landed,
    reduced,
    final,
    sums,
    sums_in,
    outgoing,
    load_sem,
    swap_send,
    swap_recv,
    init_send,
    init_recv,
    meta_send,
    meta_recv,
    ag_send,
    ag_recv,
    rs_send,
    rs_recv,
    fin_send,
    fin_recv,
    gw_send,
    gw_recv,
    out_sem,
):
    p = lax.axis_index("phase")
    tp = lax.axis_index("tp")
    d = lax.axis_index("dp")
    c = tp // 2
    k = tp % 2
    mirror = PHASES - 1 - p
    has_next = p < PHASES - 1
    has_last = p > 0
    index1 = jnp.where(k == 0, p, mirror)
    back = jnp.maximum(p - 1, 0)
    index2 = jnp.where(k == 0, back, PHASES - 1 - back)

    def remote(src, dst, send, recv, device):
        return pltpu.make_async_remote_copy(
            src_ref=src,
            dst_ref=dst,
            send_sem=send,
            recv_sem=recv,
            device_id=device,
            device_id_type=MESH,
        )

    def peer(phase, rep, m):
        other = 2 * (c ^ m) + k
        return (phase, other, d if rep == 0 else 1 - d)

    core_mate = (p, 2 * c + 1 - k, d)

    loads = [
        pltpu.make_async_copy(w_qkv, wq.at[0], load_sem.at[0]),
        pltpu.make_async_copy(w_out, wo.at[0], load_sem.at[1]),
    ]
    for copy in loads:
        copy.start()

    barrier = pltpu.get_barrier_semaphore()

    def greet(device):
        pl.semaphore_signal(barrier, inc=1, device_id=device, device_id_type=MESH)

    greet(core_mate)
    for m in range(1, CHIPS):
        greet(peer(p, 0, m))
    for m in range(CHIPS):
        greet(peer(p, 1, m))
    greet((mirror, 2 * c + 1, d))

    @pl.when(k == 1)
    def _():
        greet((mirror, 2 * c, d))

    @pl.when(has_last)
    def _():
        for rep in range(2):
            for m in range(CHIPS):
                greet(peer(p - 1, rep, m))

    @pl.when(has_next)
    def _():
        for rep in range(2):
            for m in range(CHIPS):
                greet(peer(p + 1, rep, m))

    expected = (
        8
        + 1
        + k
        + 8 * jnp.where(has_next, 1, 0)
        + 8 * jnp.where(has_last, 1, 0)
    )

    eye = identity(SHARD)
    for i, ref in enumerate((down_x, up_x, down_cot, up_cot)):
        staged[i] = dot_nt(eye, ref[...]).astype(BF16)
    for tick, index in enumerate((index1, index2)):
        for i, table in enumerate((segments, patch_rows, patch_cols)):
            meta[0, tick, pl.ds(i, 1), :] = table[k, 0, pl.ds(index, 1), :]
        meta[0, tick, 3:8, :] = jnp.zeros((5, TOK), jnp.int32)

    pl.semaphore_wait(barrier, expected)

    def rows_at(start, size):
        return pl.ds(pl.multiple_of(start, SHARD), size)

    full_in = (x1, g2)
    down_init = []
    up_init = []
    for i in range(2):
        spot = full_in[i].at[0, rows_at(c * CHUNK + k * SHARD, SHARD), :]
        up_init.append(
            remote(
                staged.at[2 * i + 1],
                spot,
                init_send.at[i, 0],
                init_recv.at[i, k],
                (mirror, 2 * c + 1, d),
            )
        )
        down_init.append(
            remote(
                staged.at[2 * i],
                spot,
                init_send.at[i, 1],
                init_recv.at[i, k],
                (p, 2 * c, d),
            )
        )
    for i in range(2):
        up_init[i].start()

        @pl.when(k == 1)
        def _():
            down_init[i].start()

        @pl.when(k == 0)
        def _():
            full_in[i][0, rows_at(c * CHUNK, SHARD), :] = staged[2 * i]

    swaps = [
        remote(w_qkv, wq.at[1], swap_send.at[0], swap_recv.at[0], core_mate),
        remote(w_out, wo.at[1], swap_send.at[1], swap_recv.at[1], core_mate),
    ]
    for copy in swaps:
        copy.start()
    meta_copy = remote(meta.at[0], meta.at[1], meta_send, meta_recv, peer(p, 1, 0))
    meta_copy.start()

    def await_init(i):
        def landing(shard):
            spot = full_in[i].at[0, rows_at(c * CHUNK + shard * SHARD, SHARD), :]
            remote(
                staged.at[0], spot, init_send.at[i, 0], init_recv.at[i, shard], core_mate
            ).wait_recv()

        @pl.when(k == 1)
        def _():
            landing(0)

        landing(1)

    def chunk_of(buffer, rep, chip):
        return buffer.at[rep, rows_at(chip * CHUNK, CHUNK), :]

    def gather(n, source, buffer, phase, rep, with_self):
        return [
            remote(
                source,
                chunk_of(buffer, rep, c),
                ag_send.at[n, rep, m],
                ag_recv.at[n, rep, m],
                peer(phase, rep, m),
            )
            for m in (3, 2, 1, 0)
            if m or rep or with_self
        ]

    def await_gather(n, buffer, rep, with_self):
        for m in range(CHIPS):
            if m or rep or with_self:
                remote(
                    reduced.at[0],
                    chunk_of(buffer, rep, c ^ m),
                    ag_send.at[n, rep, m],
                    ag_recv.at[n, rep, m],
                    core_mate,
                ).wait_recv()

    def start(copies):
        for copy in copies:
            copy.start()

    def tables(tick, rep):
        n = 2 * tick + rep
        row = lax.broadcasted_iota(jnp.int32, (HD, TOK), 0)
        power = (row % QUARTER).astype(F32)
        frequency = jnp.exp(power * (-math.log(10000.0) / QUARTER))
        position = jnp.where(
            row < 2 * QUARTER,
            jnp.broadcast_to(meta[rep, tick, 1:2, :], (HD, TOK)),
            jnp.broadcast_to(meta[rep, tick, 2:3, :], (HD, TOK)),
        ).astype(F32)
        angle = position * frequency
        first = (row < QUARTER) | ((row >= 2 * QUARTER) & (row < 3 * QUARTER))
        cosine[n] = jnp.cos(angle)
        turned = jnp.sin(angle)
        sine[n] = jnp.where(first, -turned, turned)
        ids = jnp.broadcast_to(meta[rep, tick, 0:1, :].astype(F32), (TOK, TOK))
        mask[n] = jnp.where(ids == ids.T, 1.0, 0.0)

    def flip_weights(slot):
        small = identity(TOK)

        def body(j, _):
            at = pl.ds(pl.multiple_of(j * TOK, TOK), TOK)
            wq_t[slot, at, :] = dot_nt(small, wq[slot, :, at]).astype(BF16)
            wo_t[slot, at, :] = dot_nt(small, wo[slot, :, at]).astype(BF16)
            return 0

        lax.fori_loop(0, D // TOK, body, 0)

    scale = 1.0 / math.sqrt(HD)

    def forward_head(n, slot, head):
        at = head * HD
        yq, sq = normalize(project[slot, at : at + HD, :])
        yk, sk = normalize(project[slot, SHARD + at : SHARD + at + HD, :])
        v = project[slot, 2 * SHARD + at : 2 * SHARD + at + HD, :].astype(BF16)
        qr = (yq * cosine[n] + swap_pairs(yq) * sine[n]).astype(BF16)
        kr = (yk * cosine[n] + swap_pairs(yk) * sine[n]).astype(BF16)
        raised = jnp.where(mask[n] > 0.5, jnp.exp(dot_tn(kr, qr) * scale), 0.0)
        soft = raised / jnp.sum(raised, axis=0, keepdims=True)
        blended = dot_nn(v, soft.astype(BF16))
        return yq, sq, yk, sk, qr, kr, v, soft, blended.astype(BF16)

    def backward_head(n, state, grad):
        yq, sq, yk, sk, qr, kr, v, soft = state
        gb = grad.astype(BF16)
        d_soft = dot_tn(v, gb)
        mean = jnp.sum(soft * d_soft, axis=0, keepdims=True)
        d_score = (soft * (d_soft - mean)).astype(BF16)
        dv = dot_nt(gb, soft.astype(BF16))
        dq = dot_nn(kr, d_score) * scale
        dk = dot_nt(qr, d_score) * scale
        dq = dq * cosine[n] - swap_pairs(dq) * sine[n]
        dk = dk * cosine[n] - swap_pairs(dk) * sine[n]
        dq = pull_normalize(dq, yq, sq)
        dk = pull_normalize(dk, yk, sk)
        return dq.astype(BF16), dk.astype(BF16), dv.astype(BF16)

    def run_project(buffer, rep):
        x = buffer[rep]
        for slot in range(2):
            project[slot] = dot_nn(wq[slot], x)

    def run_grad_o(buffer, rep):
        g = buffer[rep]
        for slot in range(2):
            grad_o[slot] = dot_nn(wo[slot], g)

    def forward_first(rep):
        run_project(x1, rep)

        def body(slot, _):
            for head in range(2):
                yq, sq, yk, sk, qr, kr, v, soft, o = forward_head(rep, slot, head)
                ys[rep, slot, head, 0] = yq
                ys[rep, slot, head, 1] = yk
                scales[rep, slot, head, 0:1, :] = sq
                scales[rep, slot, head, 1:2, :] = sk
                qkv[rep, slot, head, 0] = qr
                qkv[rep, slot, head, 1] = kr
                qkv[rep, slot, head, 2] = v
                weights[rep, slot, head] = soft
                heads1[rep, slot, head * HD : (head + 1) * HD, :] = o
            return 0

        lax.fori_loop(0, 2, body, 0)

    def keep(buffer, rep, slot, head, grads):
        for i in range(3):
            at = i * SHARD + head * HD
            buffer[rep, slot, at : at + HD, :] = grads[i]

    def both_second(rep):
        run_project(x2, rep)

        def body(slot, _):
            for head in range(2):
                values = forward_head(2 + rep, slot, head)
                heads2[rep, slot, head * HD : (head + 1) * HD, :] = values[8]
                grad = grad_o[slot, head * HD : (head + 1) * HD, :]
                keep(dp2, rep, slot, head, backward_head(2 + rep, values[:8], grad))
            return 0

        lax.fori_loop(0, 2, body, 0)

    def backward_first(rep):
        def body(slot, _):
            for head in range(2):
                state = (
                    ys[rep, slot, head, 0],
                    scales[rep, slot, head, 0:1, :],
                    ys[rep, slot, head, 1],
                    scales[rep, slot, head, 1:2, :],
                    qkv[rep, slot, head, 0],
                    qkv[rep, slot, head, 1],
                    qkv[rep, slot, head, 2],
                    weights[rep, slot, head],
                )
                grad = grad_o[slot, head * HD : (head + 1) * HD, :]
                keep(dp1, rep, slot, head, backward_head(rep, state, grad))
            return 0

        lax.fori_loop(0, 2, body, 0)

    def send_partials(n, flipped, small):
        copies = []
        for m in (3, 2, 1, 0):
            at = rows_at((c ^ m) * CHUNK, CHUNK)
            total = dot_nn(flipped[0, at, :], small[0, 0]) + dot_nn(
                flipped[1, at, :], small[0, 1]
            )
            if m == 0:
                partial[n, 0] = total
            else:
                outgoing[n, m - 1] = total.astype(BF16)
                copies.append(
                    remote(
                        outgoing.at[n, m - 1],
                        landed.at[n, m - 1],
                        rs_send.at[n, m - 1],
                        rs_recv.at[n, m - 1],
                        peer(p, 0, m),
                    )
                )
                copies[-1].start()
        return copies

    def reduce_partials(n, copies, residual):
        total = residual[0, rows_at(c * CHUNK, CHUNK), :].astype(F32) + partial[n, 0]
        for copy in copies:
            copy.wait_recv()
        for m in range(1, CHIPS):
            total = total + landed[n, m - 1].astype(F32)
        reduced[n] = total.astype(BF16)

    await_init(0)
    chunk = chunk_of(x1, 0, c)
    x1_own = gather(0, chunk, x1, p, 0, False)
    start(x1_own)
    tables(0, 0)
    for copy in loads:
        copy.wait()
    flip_weights(0)
    await_init(1)
    cot_chunk = chunk_of(g2, 0, c)
    cot_own = gather(1, cot_chunk, g2, p, 0, False)
    start(cot_own)
    for copy in swaps:
        copy.wait_recv()
    flip_weights(1)
    await_gather(0, x1, 0, False)
    forward_first(0)
    rs1 = send_partials(0, wo_t, heads1)
    x1_other = gather(0, chunk, x1, p, 1, False)
    start(x1_other)
    meta_copy.wait_recv()
    tables(1, 0)
    tables(0, 1)
    tables(1, 1)
    reduce_partials(0, rs1, x1)

    x2_own = gather(2, reduced.at[0], x2, p + 1, 0, True)
    x2_other = gather(2, reduced.at[0], x2, p + 1, 1, True)

    @pl.when(has_next)
    def _():
        start(x2_own)

    cot_other = gather(1, cot_chunk, g2, p, 1, False)
    start(cot_other)

    @pl.when(has_next)
    def _():
        start(x2_other)

    await_gather(0, x1, 1, False)
    forward_first(1)
    await_gather(1, g2, 0, False)
    run_grad_o(g2, 0)

    @pl.when(has_last)
    def _():
        await_gather(2, x2, 0, True)

    @pl.when(p == 0)
    def _():
        x2[...] = jnp.zeros_like(x2)

    both_second(0)
    rs2 = send_partials(1, wq_t, dp2)

    await_gather(1, g2, 1, False)
    run_grad_o(g2, 1)

    @pl.when(has_last)
    def _():
        await_gather(2, x2, 1, True)

    both_second(1)
    reduce_partials(1, rs2, g2)
    g1_own = gather(3, reduced.at[1], g1, p - 1, 0, True)
    g1_other = gather(3, reduced.at[1], g1, p - 1, 1, True)

    @pl.when(has_last)
    def _():
        start(g1_own)
        start(g1_other)

    def gradient(slot, j, tick):
        dps, xs = (dp1, x1) if tick == 0 else (dp2, x2)
        at = pl.ds(pl.multiple_of(j * SHARD, SHARD), SHARD)
        left = jnp.concatenate([dps[0, slot, at, :], dps[1, slot, at, :]], axis=1)
        right = jnp.concatenate([xs[0], xs[1]], axis=1)
        return dot_nt(left, right)

    def gradient_out(slot, tick):
        hs, gs = (heads1, g1) if tick == 0 else (heads2, g2)
        left = jnp.concatenate([hs[0, slot], hs[1, slot]], axis=1)
        right = jnp.concatenate([gs[0], gs[1]], axis=1)
        return dot_nt(left, right)

    def second_sums(i, _):
        slot = i // 3
        j = i % 3
        sums[slot, j] = gradient(slot, j, 1)
        return 0

    lax.fori_loop(0, 6, second_sums, 0)
    for slot in range(2):
        sums[slot, 3] = gradient_out(slot, 1)

    @pl.when(has_next)
    def _():
        await_gather(3, g1, 0, True)

    @pl.when(p == PHASES - 1)
    def _():
        g1[...] = jnp.zeros_like(g1)

    run_grad_o(g1, 0)
    backward_first(0)
    rs3 = send_partials(2, wq_t, dp1)

    @pl.when(has_next)
    def _():
        await_gather(3, g1, 1, True)

    run_grad_o(g1, 1)
    backward_first(1)
    reduce_partials(2, rs3, g1)

    up_fin = [
        remote(
            reduced.at[2, pl.ds(s * SHARD, SHARD), :],
            final.at[1],
            fin_send.at[s],
            fin_recv.at[1],
            (mirror, 2 * c + s, d),
        )
        for s in range(2)
    ]
    down_fin = remote(
        reduced.at[2, pl.ds(SHARD, SHARD), :], final.at[0], fin_send.at[0], fin_recv.at[0], core_mate
    )

    @pl.when(k == 1)
    def _():
        start(up_fin)

    @pl.when(k == 0)
    def _():
        down_fin.start()
        final[0] = reduced[2, 0:SHARD, :]

    handed = [
        remote(sums_in.at[0, j], sums_in.at[1, j], gw_send.at[j], gw_recv.at[j], core_mate)
        for j in range(4)
    ]
    for j in range(4):
        more = gradient(1, j, 0) if j < 3 else gradient_out(1, 0)
        sums_in[0, j] = (sums[1, j] + more).astype(BF16)
        handed[j].start()
    results = []
    for j in range(4):
        more = gradient(0, j, 0) if j < 3 else gradient_out(0, 0)
        total = sums[0, j] + more
        handed[j].wait_recv()
        sums_in[2, j] = (total + sums_in[1, j].astype(F32)).astype(BF16)
        target = out_qkv.at[pl.ds(j * SHARD, SHARD), :] if j < 3 else out_wo
        results.append(pltpu.make_async_copy(sums_in.at[2, j], target, out_sem.at[j]))
        results[-1].start()

    @pl.when(k == 1)
    def _():
        remote(staged.at[0], final.at[0], fin_send.at[0], fin_recv.at[0], core_mate).wait_recv()

    remote(staged.at[0], final.at[1], fin_send.at[0], fin_recv.at[1], core_mate).wait_recv()
    small = identity(TOK)
    out_down[...] = dot_nt(small, final[0]).astype(BF16)
    out_up[...] = dot_nt(small, final[1]).astype(BF16)

    for copy in up_init + swaps + [meta_copy] + x1_own + x1_other + cot_own + cot_other:
        copy.wait_send()
    for copy in rs1 + rs2 + rs3 + handed:
        copy.wait_send()

    @pl.when(k == 1)
    def _():
        for copy in down_init + up_fin:
            copy.wait_send()

    @pl.when(k == 0)
    def _():
        down_fin.wait_send()

    @pl.when(has_next)
    def _():
        for copy in x2_own + x2_other:
            copy.wait_send()

    @pl.when(has_last)
    def _():
        for copy in g1_own + g1_other:
            copy.wait_send()

    for copy in results:
        copy.wait()


def per_device(
    down_inputs, up_inputs, down_cot, up_cot, segment_ids, patch_rows, patch_cols, w_qkv, w_out
):
    vmem = pl.BlockSpec(memory_space=pltpu.VMEM)
    hbm = pl.BlockSpec(memory_space=pl.ANY)
    dma = pltpu.SemaphoreType.DMA
    tok_block = jax.ShapeDtypeStruct((TOK, SHARD), BF16)
    outs = pl.pallas_call(
        kernel,
        out_shape=(
            tok_block,
            tok_block,
            jax.ShapeDtypeStruct((ROWS, D), BF16),
            jax.ShapeDtypeStruct((SHARD, D), BF16),
        ),
        in_specs=[vmem] * 7 + [hbm] * 2,
        out_specs=(vmem, vmem, hbm, hbm),
        scratch_shapes=[
            pltpu.VMEM((4, SHARD, TOK), BF16),
            pltpu.VMEM((2, 2, 8, TOK), jnp.int32),
            pltpu.VMEM((4, HD, TOK), F32),
            pltpu.VMEM((4, HD, TOK), F32),
            pltpu.VMEM((4, TOK, TOK), F32),
            pltpu.VMEM((2, ROWS, D), BF16),
            pltpu.VMEM((2, SHARD, D), BF16),
            pltpu.VMEM((2, D, ROWS), BF16),
            pltpu.VMEM((2, D, SHARD), BF16),
            pltpu.VMEM((2, D, TOK), BF16),
            pltpu.VMEM((2, D, TOK), BF16),
            pltpu.VMEM((2, D, TOK), BF16),
            pltpu.VMEM((2, D, TOK), BF16),
            pltpu.VMEM((2, ROWS, TOK), F32),
            pltpu.VMEM((2, SHARD, TOK), F32),
            pltpu.VMEM((2, 2, 2, 2, HD, TOK), F32),
            pltpu.VMEM((2, 2, 2, 8, TOK), F32),
            pltpu.VMEM((2, 2, 2, 3, HD, TOK), BF16),
            pltpu.VMEM((2, 2, 2, TOK, TOK), F32),
            pltpu.VMEM((2, 2, SHARD, TOK), BF16),
            pltpu.VMEM((2, 2, SHARD, TOK), BF16),
            pltpu.VMEM((2, 2, ROWS, TOK), BF16),
            pltpu.VMEM((2, 2, ROWS, TOK), BF16),
            pltpu.VMEM((3, 1, CHUNK, TOK), F32),
            pltpu.VMEM((3, 3, CHUNK, TOK), BF16),
            pltpu.VMEM((3, CHUNK, TOK), BF16),
            pltpu.VMEM((2, SHARD, TOK), BF16),
            pltpu.VMEM((2, 4, SHARD, D), F32),
            pltpu.VMEM((3, 4, SHARD, D), BF16),
            pltpu.VMEM((3, 3, CHUNK, TOK), BF16),
            dma((2,)),
            dma((2,)),
            dma((2,)),
            dma((2, 2)),
            dma((2, 2)),
            dma,
            dma,
            dma((4, 2, 4)),
            dma((4, 2, 4)),
            dma((3, 3)),
            dma((3, 3)),
            dma((2,)),
            dma((2,)),
            dma((4,)),
            dma((4,)),
            dma((4,)),
        ],
        compiler_params=pltpu.CompilerParams(
            collective_id=0, has_side_effects=True, vmem_limit_bytes=48 << 20
        ),
    )(
        down_inputs[0, 0],
        up_inputs[0, 0],
        down_cot[0, 0],
        up_cot[0, 0],
        segment_ids,
        patch_rows,
        patch_cols,
        w_qkv.reshape(ROWS, D),
        w_out[0],
    )
    return (
        outs[0][None, None],
        outs[1][None, None],
        outs[2].reshape(w_qkv.shape),
        outs[3][None],
    )


def solution(mesh):
    return jax.shard_map(
        per_device,
        mesh=mesh,
        in_specs=(
            P("dp", "phase", None, "tp"),
            P("dp", "phase", None, "tp"),
            P("dp", "phase", None, "tp"),
            P("dp", "phase", None, "tp"),
            P(None, "dp", None, None),
            P(None, "dp", None, None),
            P(None, "dp", None, None),
            P("phase", None, "tp", None),
            P("phase", "tp", None),
        ),
        out_specs=(
            P("dp", "phase", None, "tp"),
            P("dp", "phase", None, "tp"),
            P("phase", None, "tp", None),
            P("phase", "tp", None),
        ),
        check_vma=False,
    )
```

```python
import functools
import math

import jax
import jax.numpy as jnp
from jax import lax
from jax.experimental import pallas as pl
from jax.experimental.pallas import tpu as pltpu
from jax.sharding import PartitionSpec as P

HD = 80
QUARTER = 20
TOK = 128
D = 1280
SHARD = 160
CHUNK = 320
CHIPS = 4
HEADS = 4
PHASES = 32
ROWS = 480
MESH = pl.DeviceIdType.MESH
F32 = jnp.float32
BF16 = jnp.bfloat16


def dot_nn(a, b):
    return lax.dot_general(a, b, (((1,), (0,)), ((), ())), preferred_element_type=F32)


def dot_nt(a, b):
    return lax.dot_general(a, b, (((1,), (1,)), ((), ())), preferred_element_type=F32)


def dot_tn(a, b):
    return lax.dot_general(a, b, (((0,), (0,)), ((), ())), preferred_element_type=F32)


def normalize(x):
    centred = x - jnp.mean(x, axis=0, keepdims=True)
    scale = lax.rsqrt(jnp.mean(centred * centred, axis=0, keepdims=True) + 1e-06)
    return centred * scale, scale


def pull_normalize(grad, y, scale):
    return scale * (
        grad
        - jnp.mean(grad, axis=0, keepdims=True)
        - y * jnp.mean(grad * y, axis=0, keepdims=True)
    )


def swap_pairs(y):
    row = lax.broadcasted_iota(jnp.int32, y.shape, 0)
    first = (row < QUARTER) | ((row >= 2 * QUARTER) & (row < 3 * QUARTER))
    return jnp.where(first, pltpu.roll(y, HD - QUARTER, axis=0), pltpu.roll(y, QUARTER, axis=0))


def identity(size):
    row = lax.broadcasted_iota(jnp.int32, (size, size), 0)
    column = lax.broadcasted_iota(jnp.int32, (size, size), 1)
    return jnp.where(row == column, 1.0, 0.0).astype(BF16)


def kernel(
    down_x,
    up_x,
    down_cot,
    up_cot,
    segments,
    patch_rows,
    patch_cols,
    w_qkv,
    w_out,
    out_down,
    out_up,
    out_qkv,
    out_wo,
    tables_in,
    meta,
    cosine,
    sine,
    mask,
    wq,
    wo,
    wq_t,
    wo_t,
    x1,
    x2,
    g1,
    g2,
    project,
    grad_o,
    ys,
    scales,
    qkv,
    weights,
    heads1,
    heads2,
    dp1,
    dp2,
    partial,
    landed,
    reduced,
    final,
    sums,
    sums_in,
    outgoing,
    load_sem,
    swap_send,
    swap_recv,
    init_send,
    init_recv,
    meta_send,
    meta_recv,
    ag_send,
    ag_recv,
    relay_send,
    relay_recv,
    rs_send,
    rs_recv,
    fin_send,
    fin_recv,
    gw_send,
    gw_recv,
    out_sem,
):
    p = lax.axis_index("phase")
    tp = lax.axis_index("tp")
    d = lax.axis_index("dp")
    c = tp // 2
    k = tp % 2
    mirror = PHASES - 1 - p
    has_next = p < PHASES - 1
    has_last = p > 0
    index1 = jnp.where(k == 0, p, mirror)
    back = jnp.maximum(p - 1, 0)
    index2 = jnp.where(k == 0, back, PHASES - 1 - back)

    def remote(src, dst, send, recv, device):
        return pltpu.make_async_remote_copy(
            src_ref=src,
            dst_ref=dst,
            send_sem=send,
            recv_sem=recv,
            device_id=device,
            device_id_type=MESH,
        )

    def peer(phase, rep, m):
        other = 2 * (c ^ m) + k
        return (phase, other, d if rep == 0 else 1 - d)

    core_mate = (p, 2 * c + 1 - k, d)

    def start(copies):
        for copy in copies:
            copy.start()

    loads = [
        pltpu.make_async_copy(w_qkv, wq.at[0], load_sem.at[0]),
        pltpu.make_async_copy(w_out, wo.at[0], load_sem.at[1]),
    ]
    for copy in loads:
        copy.start()

    barrier = pltpu.get_barrier_semaphore()

    def greet(device):
        pl.semaphore_signal(barrier, inc=1, device_id=device, device_id_type=MESH)

    greet(core_mate)
    for m in range(1, CHIPS):
        greet(peer(p, 0, m))
    for m in range(CHIPS):
        greet(peer(p, 1, m))
    greet((mirror, 2 * c + 1, d))

    @pl.when(k == 1)
    def _():
        greet((mirror, 2 * c, d))

    @pl.when(has_last)
    def _():
        for m in range(CHIPS):
            greet(peer(p - 1, 0, m))

    @pl.when(has_next)
    def _():
        for rep in range(2):
            for m in range(CHIPS):
                greet(peer(p + 1, rep, m))

    expected = (
        8
        + 1
        + k
        + 4 * jnp.where(has_next, 1, 0)
        + 8 * jnp.where(has_last, 1, 0)
    )

    table_loads = [
        pltpu.make_async_copy(table.at[k, 0], tables_in.at[i], load_sem.at[2 + i])
        for i, table in enumerate((segments, patch_rows, patch_cols))
    ]
    for copy in table_loads:
        copy.start()

    pl.semaphore_wait(barrier, expected)

    def rows_at(start, size):
        return pl.ds(pl.multiple_of(start, SHARD), size)

    full_in = (x1, g2)
    downs = (down_x, down_cot)
    ups = (up_x, up_cot)
    down_init = []
    up_init = []
    down_local = []
    for i in range(2):
        spot = full_in[i].at[0, rows_at(c * CHUNK + k * SHARD, SHARD), :]
        up_init.append(
            remote(
                ups[i],
                spot,
                init_send.at[i, 0],
                init_recv.at[i, k],
                (mirror, 2 * c + 1, d),
            )
        )
        down_init.append(
            remote(
                downs[i],
                spot,
                init_send.at[i, 1],
                init_recv.at[i, k],
                (p, 2 * c, d),
            )
        )
        down_local.append(
            pltpu.make_async_copy(
                downs[i], full_in[i].at[0, rows_at(c * CHUNK, SHARD), :], load_sem.at[5 + i]
            )
        )
    for i in range(2):
        up_init[i].start()

        @pl.when(k == 1)
        def _():
            down_init[i].start()

        @pl.when(k == 0)
        def _():
            down_local[i].start()

    swaps = [
        remote(w_qkv, wq.at[1], swap_send.at[0], swap_recv.at[0], core_mate),
        remote(w_out, wo.at[1], swap_send.at[1], swap_recv.at[1], core_mate),
    ]
    @pl.when(k == 1)
    def _():
        start(swaps)

    for copy in table_loads:
        copy.wait()
    for tick, index in enumerate((index1, index2)):
        for i in range(3):
            meta[0, tick, pl.ds(i, 1), :] = tables_in[i, pl.ds(index, 1), :]
        meta[0, tick, 3:8, :] = jnp.zeros((5, TOK), jnp.int32)
    meta_copy = remote(meta.at[0], meta.at[1], meta_send, meta_recv, peer(p, 1, 0))
    meta_copy.start()

    def await_init(i):
        def landing(shard):
            spot = full_in[i].at[0, rows_at(c * CHUNK + shard * SHARD, SHARD), :]
            remote(
                downs[0], spot, init_send.at[i, 0], init_recv.at[i, shard], core_mate
            ).wait_recv()

        @pl.when(k == 1)
        def _():
            landing(0)

        @pl.when(k == 0)
        def _():
            down_local[i].wait()

        landing(1)

    def chunk_of(buffer, rep, chip):
        return buffer.at[rep, rows_at(chip * CHUNK, CHUNK), :]

    def gather(n, source, buffer, phase, rep, with_self):
        return [
            remote(
                source,
                chunk_of(buffer, rep, c),
                ag_send.at[n, rep, m],
                ag_recv.at[n, rep, m],
                peer(phase, rep, m),
            )
            for m in (3, 2, 1, 0)
            if m or rep or with_self
        ]

    def await_gather(n, buffer, rep, with_self):
        for m in range(CHIPS):
            if m or rep or with_self:
                remote(
                    reduced.at[0],
                    chunk_of(buffer, rep, c ^ m),
                    ag_send.at[n, rep, m],
                    ag_recv.at[n, rep, m],
                    core_mate,
                ).wait_recv()

    def tables(tick, rep):
        n = 2 * tick + rep
        row = lax.broadcasted_iota(jnp.int32, (HD, TOK), 0)
        power = (row % QUARTER).astype(F32)
        frequency = jnp.exp(power * (-math.log(10000.0) / QUARTER))
        position = jnp.where(
            row < 2 * QUARTER,
            jnp.broadcast_to(meta[rep, tick, 1:2, :], (HD, TOK)),
            jnp.broadcast_to(meta[rep, tick, 2:3, :], (HD, TOK)),
        ).astype(F32)
        angle = position * frequency
        first = (row < QUARTER) | ((row >= 2 * QUARTER) & (row < 3 * QUARTER))
        cosine[n] = jnp.cos(angle)
        turned = jnp.sin(angle)
        sine[n] = jnp.where(first, -turned, turned)
        ids = jnp.broadcast_to(meta[rep, tick, 0:1, :].astype(F32), (TOK, TOK))
        mask[n] = jnp.where(ids == ids.T, 1.0, 0.0)

    def flip_weights(slot):
        small = identity(TOK)

        def body(j, _):
            at = pl.ds(pl.multiple_of(j * TOK, TOK), TOK)
            wq_t[slot, at, :] = dot_nt(small, wq[slot, :, at]).astype(BF16)
            wo_t[slot, at, :] = dot_nt(small, wo[slot, :, at]).astype(BF16)
            return 0

        lax.fori_loop(0, D // TOK, body, 0)

    scale = 1.0 / math.sqrt(HD)

    def forward_head(n, slot, head):
        at = head * HD
        yq, sq = normalize(project[slot, at : at + HD, :])
        yk, sk = normalize(project[slot, SHARD + at : SHARD + at + HD, :])
        v = project[slot, 2 * SHARD + at : 2 * SHARD + at + HD, :].astype(BF16)
        qr = (yq * cosine[n] + swap_pairs(yq) * sine[n]).astype(BF16)
        kr = (yk * cosine[n] + swap_pairs(yk) * sine[n]).astype(BF16)
        raised = jnp.where(mask[n] > 0.5, jnp.exp(dot_tn(kr, qr) * scale), 0.0)
        soft = raised / jnp.sum(raised, axis=0, keepdims=True)
        blended = dot_nn(v, soft.astype(BF16))
        return yq, sq, yk, sk, qr, kr, v, soft, blended.astype(BF16)

    def backward_head(n, state, grad):
        yq, sq, yk, sk, qr, kr, v, soft = state
        gb = grad.astype(BF16)
        d_soft = dot_tn(v, gb)
        mean = jnp.sum(soft * d_soft, axis=0, keepdims=True)
        d_score = (soft * (d_soft - mean)).astype(BF16)
        dv = dot_nt(gb, soft.astype(BF16))
        dq = dot_nn(kr, d_score) * scale
        dk = dot_nt(qr, d_score) * scale
        dq = dq * cosine[n] - swap_pairs(dq) * sine[n]
        dk = dk * cosine[n] - swap_pairs(dk) * sine[n]
        dq = pull_normalize(dq, yq, sq)
        dk = pull_normalize(dk, yk, sk)
        return dq.astype(BF16), dk.astype(BF16), dv.astype(BF16)

    def run_project(buffer, rep):
        x = buffer[rep]
        for slot in range(2):
            project[slot] = dot_nn(wq[slot], x)

    def run_grad_o(buffer, rep):
        g = buffer[rep]
        for slot in range(2):
            grad_o[slot] = dot_nn(wo[slot], g)

    def forward_first(rep):
        run_project(x1, rep)

        def body(slot, _):
            for head in range(2):
                yq, sq, yk, sk, qr, kr, v, soft, o = forward_head(rep, slot, head)
                ys[rep, slot, head, 0] = yq
                ys[rep, slot, head, 1] = yk
                scales[rep, slot, head, 0:1, :] = sq
                scales[rep, slot, head, 1:2, :] = sk
                qkv[rep, slot, head, 0] = qr
                qkv[rep, slot, head, 1] = kr
                qkv[rep, slot, head, 2] = v
                weights[rep, slot, head] = soft
                heads1[rep, slot, head * HD : (head + 1) * HD, :] = o
            return 0

        lax.fori_loop(0, 2, body, 0)

    def keep(buffer, rep, slot, head, grads):
        for i in range(3):
            at = i * SHARD + head * HD
            buffer[rep, slot, at : at + HD, :] = grads[i]

    def both_second(rep):
        run_project(x2, rep)

        def body(slot, _):
            for head in range(2):
                values = forward_head(2 + rep, slot, head)
                heads2[rep, slot, head * HD : (head + 1) * HD, :] = values[8]
                grad = grad_o[slot, head * HD : (head + 1) * HD, :]
                keep(dp2, rep, slot, head, backward_head(2 + rep, values[:8], grad))
            return 0

        lax.fori_loop(0, 2, body, 0)

    def backward_first(rep):
        def body(slot, _):
            for head in range(2):
                state = (
                    ys[rep, slot, head, 0],
                    scales[rep, slot, head, 0:1, :],
                    ys[rep, slot, head, 1],
                    scales[rep, slot, head, 1:2, :],
                    qkv[rep, slot, head, 0],
                    qkv[rep, slot, head, 1],
                    qkv[rep, slot, head, 2],
                    weights[rep, slot, head],
                )
                grad = grad_o[slot, head * HD : (head + 1) * HD, :]
                keep(dp1, rep, slot, head, backward_head(rep, state, grad))
            return 0

        lax.fori_loop(0, 2, body, 0)

    def send_partials(n, flipped, small):
        copies = []
        for m in (3, 2, 1, 0):
            at = rows_at((c ^ m) * CHUNK, CHUNK)
            total = dot_nn(flipped[0, at, :], small[0, 0]) + dot_nn(
                flipped[1, at, :], small[0, 1]
            )
            if m == 0:
                partial[n, 0] = total
            else:
                outgoing[n, m - 1] = total.astype(BF16)
                copies.append(
                    remote(
                        outgoing.at[n, m - 1],
                        landed.at[n, m - 1],
                        rs_send.at[n, m - 1],
                        rs_recv.at[n, m - 1],
                        peer(p, 0, m),
                    )
                )
                copies[-1].start()
        return copies

    def reduce_partials(n, copies, residual):
        total = residual[0, rows_at(c * CHUNK, CHUNK), :].astype(F32) + partial[n, 0]
        for copy in copies:
            copy.wait_recv()
        for m in range(1, CHIPS):
            total = total + landed[n, m - 1].astype(F32)
        reduced[n] = total.astype(BF16)

    half = 2 * CHUNK

    def relay(n, buffer):
        def piece(rep, start):
            return buffer.at[rep, pl.ds(start, half), :]

        def hand(start, chip, s):
            return remote(
                piece(0, start),
                piece(1, start),
                relay_send.at[n, s],
                relay_recv.at[n, 0],
                (p, 2 * chip + k, 1 - d),
            )

        first = [hand(0, 3, 0), hand(0, 1, 1)]
        last = [hand(half, 0, 0), hand(half, 2, 1)]
        mine = pl.multiple_of((1 - c % 2) * half, half)
        other = pl.multiple_of((c % 2) * half, half)
        onward = remote(
            piece(1, mine), piece(1, mine), relay_send.at[n, 2], relay_recv.at[n, 1], peer(p, 0, 1)
        )

        def begin():
            @pl.when(c == 0)
            def _():
                start(first)

            @pl.when(c == 3)
            def _():
                start(last)

        def forward():
            remote(
                piece(0, 0), piece(1, mine), relay_send.at[n, 0], relay_recv.at[n, 0], core_mate
            ).wait_recv()
            onward.start()

        def finish():
            remote(
                piece(0, 0), piece(1, other), relay_send.at[n, 0], relay_recv.at[n, 1], core_mate
            ).wait_recv()

        def drain():
            onward.wait_send()

            @pl.when(c == 0)
            def _():
                for copy in first:
                    copy.wait_send()

            @pl.when(c == 3)
            def _():
                for copy in last:
                    copy.wait_send()

        return begin, forward, finish, drain

    def direct(n, source, buffer, phase):
        chip = jnp.where(c >= 2, 0, 1)
        return [
            remote(
                source,
                chunk_of(buffer, 1, c),
                ag_send.at[n, 1, i],
                ag_recv.at[n, 1, c % 2],
                (phase, 2 * (chip + 2 * i) + k, 1 - d),
            )
            for i in range(2)
        ]

    def direct_relay(n, buffer):
        mine = pl.multiple_of((1 - c % 2) * half, half)
        other = pl.multiple_of((c % 2) * half, half)

        def piece(start):
            return buffer.at[1, pl.ds(start, half), :]

        onward = remote(
            piece(mine), piece(mine), relay_send.at[3, 2], relay_recv.at[3, 1], peer(p, 0, 1)
        )

        def forward():
            for i in range(2):
                remote(
                    reduced.at[0],
                    buffer.at[1, pl.ds(pl.multiple_of(mine + i * CHUNK, CHUNK), CHUNK), :],
                    ag_send.at[n, 1, i],
                    ag_recv.at[n, 1, i],
                    core_mate,
                ).wait_recv()
            onward.start()

        def finish():
            remote(
                piece(mine), piece(other), relay_send.at[3, 2], relay_recv.at[3, 1], core_mate
            ).wait_recv()

        return forward, finish, onward

    x1_relay = relay(0, x1)
    x2_relay = relay(1, x2)
    cot_relay = relay(2, g2)

    await_init(0)
    x1_own = gather(0, chunk_of(x1, 0, c), x1, p, 0, False)
    start(x1_own)

    @pl.when(k == 0)
    def _():
        start(swaps)

    tables(0, 0)
    for copy in loads:
        copy.wait()
    flip_weights(0)
    await_init(1)
    cot_own = gather(1, chunk_of(g2, 0, c), g2, p, 0, False)
    for copy in swaps:
        copy.wait_recv()
    flip_weights(1)
    await_gather(0, x1, 0, False)
    start(cot_own)
    forward_first(0)
    rs1 = send_partials(0, wo_t, heads1)
    tables(1, 0)
    meta_copy.wait_recv()
    tables(0, 1)
    tables(1, 1)
    reduce_partials(0, rs1, x1)

    x2_own = gather(2, reduced.at[0], x2, p + 1, 0, True)

    @pl.when(has_next)
    def _():
        start(x2_own)

    await_gather(1, g2, 0, False)
    run_grad_o(g2, 0)
    x1_relay[0]()

    @pl.when(has_last)
    def _():
        await_gather(2, x2, 0, True)

    @pl.when(p == 0)
    def _():
        x2[0] = jnp.zeros_like(x2[0])

    x2_relay[0]()
    cot_relay[0]()
    both_second(0)
    rs2 = send_partials(1, wq_t, dp2)
    x1_relay[1]()
    reduce_partials(1, rs2, g2)
    g1_own = gather(3, reduced.at[1], g1, p - 1, 0, True)
    g1_other = direct(3, reduced.at[1], g1, p - 1)
    g1_forward, g1_finish, g1_onward = direct_relay(3, g1)

    @pl.when(has_last)
    def _():
        start(g1_own)
        start(g1_other)

    x2_relay[1]()
    x1_relay[2]()
    forward_first(1)

    def gradient(slot, j, tick):
        dps, xs = (dp1, x1) if tick == 0 else (dp2, x2)
        at = pl.ds(pl.multiple_of(j * SHARD, SHARD), SHARD)
        left = jnp.concatenate([dps[0, slot, at, :], dps[1, slot, at, :]], axis=1)
        right = jnp.concatenate([xs[0], xs[1]], axis=1)
        return dot_nt(left, right)

    def gradient_out(slot, tick):
        hs, gs = (heads1, g1) if tick == 0 else (heads2, g2)
        left = jnp.concatenate([hs[0, slot], hs[1, slot]], axis=1)
        right = jnp.concatenate([gs[0], gs[1]], axis=1)
        return dot_nt(left, right)

    def second_sums(i, _):
        slot = i // 3
        j = i % 3
        sums[slot, j] = gradient(slot, j, 1)
        return 0

    @pl.when(has_next)
    def _():
        await_gather(3, g1, 0, True)

    @pl.when(p == PHASES - 1)
    def _():
        g1[...] = jnp.zeros_like(g1)

    cot_relay[1]()
    run_grad_o(g1, 0)
    backward_first(0)
    rs3 = send_partials(2, wq_t, dp1)

    @pl.when(has_next)
    def _():
        g1_forward()

    cot_relay[2]()
    run_grad_o(g2, 1)
    x2_relay[2]()
    both_second(1)
    lax.fori_loop(0, 6, second_sums, 0)
    for slot in range(2):
        sums[slot, 3] = gradient_out(slot, 1)
    reduce_partials(2, rs3, g1)

    up_fin = [
        remote(
            reduced.at[2, pl.ds(s * SHARD, SHARD), :],
            final.at[1],
            fin_send.at[s],
            fin_recv.at[1],
            (mirror, 2 * c + s, d),
        )
        for s in range(2)
    ]
    down_fin = remote(
        reduced.at[2, pl.ds(SHARD, SHARD), :], final.at[0], fin_send.at[0], fin_recv.at[0], core_mate
    )

    down_kept = pltpu.make_async_copy(
        reduced.at[2, pl.ds(0, SHARD), :], final.at[0], load_sem.at[7]
    )

    @pl.when(k == 1)
    def _():
        start(up_fin)

    @pl.when(k == 0)
    def _():
        down_fin.start()
        down_kept.start()

    @pl.when(has_next)
    def _():
        g1_finish()

    run_grad_o(g1, 1)
    backward_first(1)

    handed = [
        remote(sums_in.at[0, j], sums_in.at[1, j], gw_send.at[j], gw_recv.at[j], core_mate)
        for j in range(4)
    ]
    for j in range(4):
        more = gradient(1, j, 0) if j < 3 else gradient_out(1, 0)
        sums_in[0, j] = (sums[1, j] + more).astype(BF16)
        handed[j].start()
    results = []
    for j in range(4):
        more = gradient(0, j, 0) if j < 3 else gradient_out(0, 0)
        total = sums[0, j] + more
        handed[j].wait_recv()
        sums_in[2, j] = (total + sums_in[1, j].astype(F32)).astype(BF16)
        target = out_qkv.at[pl.ds(j * SHARD, SHARD), :] if j < 3 else out_wo
        results.append(pltpu.make_async_copy(sums_in.at[2, j], target, out_sem.at[j]))
        results[-1].start()

    @pl.when(k == 1)
    def _():
        remote(downs[0], final.at[0], fin_send.at[0], fin_recv.at[0], core_mate).wait_recv()

    @pl.when(k == 0)
    def _():
        down_kept.wait()

    remote(downs[0], final.at[1], fin_send.at[0], fin_recv.at[1], core_mate).wait_recv()
    for i, target in enumerate((out_down, out_up)):
        results.append(pltpu.make_async_copy(final.at[i], target, out_sem.at[4 + i]))
        results[-1].start()

    for copy in up_init + swaps + [meta_copy] + x1_own + cot_own:
        copy.wait_send()
    for line in (x1_relay, x2_relay, cot_relay):
        line[3]()
    for copy in rs1 + rs2 + rs3 + handed:
        copy.wait_send()

    @pl.when(k == 1)
    def _():
        for copy in down_init + up_fin:
            copy.wait_send()

    @pl.when(k == 0)
    def _():
        down_fin.wait_send()

    @pl.when(has_next)
    def _():
        for copy in x2_own:
            copy.wait_send()

    @pl.when(has_last)
    def _():
        for copy in g1_own + g1_other:
            copy.wait_send()

    @pl.when(has_next)
    def _():
        g1_onward.wait_send()

    for copy in results:
        copy.wait()


def place(*refs):
    sources, targets, kept, sem = refs[:4], refs[4:8], refs[8:12], refs[12]
    pieces = []
    for i, count in enumerate((1, 1, 6, 2)):
        rows = sources[i].shape[0] // count
        pieces += [(i, pl.ds(j * rows, rows)) for j in range(count)]
    inward = [
        pltpu.make_async_copy(sources[i].at[at], kept[i].at[at], sem.at[0, n])
        for n, (i, at) in enumerate(pieces)
    ]
    outward = [
        pltpu.make_async_copy(kept[i].at[at], targets[i].at[at], sem.at[1, n])
        for n, (i, at) in enumerate(pieces)
    ]
    for copy in inward:
        copy.start()
    for before, copy in zip(inward, outward):
        before.wait()
        copy.start()
    for copy in outward:
        copy.wait()


def per_device(
    down_inputs, up_inputs, down_cot, up_cot, segment_ids, patch_rows, patch_cols, w_qkv, w_out
):
    hbm = pl.BlockSpec(memory_space=pltpu.HBM)
    dma = pltpu.SemaphoreType.DMA
    tok_block = jax.ShapeDtypeStruct((SHARD, TOK), BF16)
    shapes = (
        tok_block,
        tok_block,
        jax.ShapeDtypeStruct((ROWS, D), BF16),
        jax.ShapeDtypeStruct((SHARD, D), BF16),
    )
    outs = pl.pallas_call(
        kernel,
        out_shape=shapes,
        in_specs=[hbm] * 9,
        out_specs=(hbm,) * 4,
        scratch_shapes=[
            pltpu.VMEM((3, PHASES, TOK), jnp.int32),
            pltpu.VMEM((2, 2, 8, TOK), jnp.int32),
            pltpu.VMEM((4, HD, TOK), F32),
            pltpu.VMEM((4, HD, TOK), F32),
            pltpu.VMEM((4, TOK, TOK), F32),
            pltpu.VMEM((2, ROWS, D), BF16),
            pltpu.VMEM((2, SHARD, D), BF16),
            pltpu.VMEM((2, D, ROWS), BF16),
            pltpu.VMEM((2, D, SHARD), BF16),
            pltpu.VMEM((2, D, TOK), BF16),
            pltpu.VMEM((2, D, TOK), BF16),
            pltpu.VMEM((2, D, TOK), BF16),
            pltpu.VMEM((2, D, TOK), BF16),
            pltpu.VMEM((2, ROWS, TOK), F32),
            pltpu.VMEM((2, SHARD, TOK), F32),
            pltpu.VMEM((2, 2, 2, 2, HD, TOK), F32),
            pltpu.VMEM((2, 2, 2, 8, TOK), F32),
            pltpu.VMEM((2, 2, 2, 3, HD, TOK), BF16),
            pltpu.VMEM((2, 2, 2, TOK, TOK), F32),
            pltpu.VMEM((2, 2, SHARD, TOK), BF16),
            pltpu.VMEM((2, 2, SHARD, TOK), BF16),
            pltpu.VMEM((2, 2, ROWS, TOK), BF16),
            pltpu.VMEM((2, 2, ROWS, TOK), BF16),
            pltpu.VMEM((3, 1, CHUNK, TOK), F32),
            pltpu.VMEM((3, 3, CHUNK, TOK), BF16),
            pltpu.VMEM((3, CHUNK, TOK), BF16),
            pltpu.VMEM((2, SHARD, TOK), BF16),
            pltpu.VMEM((2, 4, SHARD, D), F32),
            pltpu.VMEM((3, 4, SHARD, D), BF16),
            pltpu.VMEM((3, 3, CHUNK, TOK), BF16),
            dma((8,)),
            dma((2,)),
            dma((2,)),
            dma((2, 2)),
            dma((2, 2)),
            dma,
            dma,
            dma((4, 2, 4)),
            dma((4, 2, 4)),
            dma((4, 3)),
            dma((4, 2)),
            dma((3, 3)),
            dma((3, 3)),
            dma((2,)),
            dma((2,)),
            dma((4,)),
            dma((4,)),
            dma((6,)),
        ],
        compiler_params=pltpu.CompilerParams(
            collective_id=0, has_side_effects=True, vmem_limit_bytes=60 << 20
        ),
    )(
        down_inputs[0, 0].T,
        up_inputs[0, 0].T,
        down_cot[0, 0].T,
        up_cot[0, 0].T,
        segment_ids,
        patch_rows,
        patch_cols,
        w_qkv.reshape(ROWS, D),
        w_out[0],
    )
    outs = pl.pallas_call(
        place,
        out_shape=shapes,
        in_specs=[hbm] * 4,
        out_specs=(hbm,) * 4,
        scratch_shapes=[pltpu.VMEM(x.shape, BF16) for x in shapes] + [dma((2, 10))],
        compiler_params=pltpu.CompilerParams(vmem_limit_bytes=60 << 20),
    )(*outs)
    return (
        outs[0].T[None, None],
        outs[1].T[None, None],
        outs[2].reshape(w_qkv.shape),
        outs[3][None],
    )


def solution(mesh):
    return jax.shard_map(
        per_device,
        mesh=mesh,
        in_specs=(
            P("dp", "phase", None, "tp"),
            P("dp", "phase", None, "tp"),
            P("dp", "phase", None, "tp"),
            P("dp", "phase", None, "tp"),
            P(None, "dp", None, None),
            P(None, "dp", None, None),
            P(None, "dp", None, None),
            P("phase", None, "tp", None),
            P("phase", "tp", None),
        ),
        out_specs=(
            P("dp", "phase", None, "tp"),
            P("dp", "phase", None, "tp"),
            P("phase", None, "tp", None),
            P("phase", "tp", None),
        ),
        check_vma=False,
    )
```

```python
import functools
import math

import jax
import jax.numpy as jnp
from jax import lax
from jax.experimental import pallas as pl
from jax.experimental.pallas import tpu as pltpu
from jax.sharding import PartitionSpec as P

HD = 80
QUARTER = 20
TOK = 128
D = 1280
SHARD = 160
CHUNK = 320
CHIPS = 4
HEADS = 4
PHASES = 32
ROWS = 480
MESH = pl.DeviceIdType.MESH
F32 = jnp.float32
BF16 = jnp.bfloat16


def dot_nn(a, b):
    return lax.dot_general(a, b, (((1,), (0,)), ((), ())), preferred_element_type=F32)


def dot_nt(a, b):
    return lax.dot_general(a, b, (((1,), (1,)), ((), ())), preferred_element_type=F32)


def dot_tn(a, b):
    return lax.dot_general(a, b, (((0,), (0,)), ((), ())), preferred_element_type=F32)


def normalize(x):
    centred = x - jnp.mean(x, axis=0, keepdims=True)
    scale = lax.rsqrt(jnp.mean(centred * centred, axis=0, keepdims=True) + 1e-06)
    return centred * scale, scale


def pull_normalize(grad, y, scale):
    return scale * (
        grad
        - jnp.mean(grad, axis=0, keepdims=True)
        - y * jnp.mean(grad * y, axis=0, keepdims=True)
    )


def swap_pairs(y):
    row = lax.broadcasted_iota(jnp.int32, y.shape, 0)
    first = (row < QUARTER) | ((row >= 2 * QUARTER) & (row < 3 * QUARTER))
    return jnp.where(first, pltpu.roll(y, HD - QUARTER, axis=0), pltpu.roll(y, QUARTER, axis=0))


def identity(size):
    row = lax.broadcasted_iota(jnp.int32, (size, size), 0)
    column = lax.broadcasted_iota(jnp.int32, (size, size), 1)
    return jnp.where(row == column, 1.0, 0.0).astype(BF16)


def kernel(
    down_x,
    up_x,
    down_cot,
    up_cot,
    segments,
    patch_rows,
    patch_cols,
    w_qkv,
    w_out,
    out_down,
    out_up,
    out_qkv,
    out_wo,
    tables_in,
    meta,
    cosine,
    sine,
    mask,
    wq,
    wo,
    wq_t,
    wo_t,
    x1,
    x2,
    g1,
    g2,
    project,
    grad_o,
    ys,
    scales,
    qkv,
    weights,
    heads1,
    heads2,
    dp1,
    dp2,
    partial,
    landed,
    reduced,
    final,
    sums,
    sums_in,
    outgoing,
    load_sem,
    swap_send,
    swap_recv,
    init_send,
    init_recv,
    meta_send,
    meta_recv,
    ag_send,
    ag_recv,
    relay_send,
    relay_recv,
    rs_send,
    rs_recv,
    fin_send,
    fin_recv,
    gw_send,
    gw_recv,
    out_sem,
):
    p = lax.axis_index("phase")
    tp = lax.axis_index("tp")
    d = lax.axis_index("dp")
    c = tp // 2
    k = tp % 2
    mirror = PHASES - 1 - p
    has_next = p < PHASES - 1
    has_last = p > 0
    index1 = jnp.where(k == 0, p, mirror)
    back = jnp.maximum(p - 1, 0)
    index2 = jnp.where(k == 0, back, PHASES - 1 - back)

    def remote(src, dst, send, recv, device):
        return pltpu.make_async_remote_copy(
            src_ref=src,
            dst_ref=dst,
            send_sem=send,
            recv_sem=recv,
            device_id=device,
            device_id_type=MESH,
        )

    def peer(phase, rep, m):
        other = 2 * (c ^ m) + k
        return (phase, other, d if rep == 0 else 1 - d)

    core_mate = (p, 2 * c + 1 - k, d)

    def start(copies):
        for copy in copies:
            copy.start()

    loads = [
        pltpu.make_async_copy(w_qkv, wq.at[0], load_sem.at[0]),
        pltpu.make_async_copy(w_out, wo.at[0], load_sem.at[1]),
    ]
    for copy in loads:
        copy.start()

    barrier = pltpu.get_barrier_semaphore()

    def greet(device):
        pl.semaphore_signal(barrier, inc=1, device_id=device, device_id_type=MESH)

    greet(core_mate)
    for m in range(1, CHIPS):
        greet(peer(p, 0, m))
    for m in range(CHIPS):
        greet(peer(p, 1, m))
    greet((mirror, 2 * c + 1, d))

    @pl.when(k == 1)
    def _():
        greet((mirror, 2 * c, d))

    @pl.when(has_last)
    def _():
        for m in range(CHIPS):
            greet(peer(p - 1, 0, m))

    @pl.when(has_next)
    def _():
        for rep in range(2):
            for m in range(CHIPS):
                greet(peer(p + 1, rep, m))

    expected = (
        8
        + 1
        + k
        + 4 * jnp.where(has_next, 1, 0)
        + 8 * jnp.where(has_last, 1, 0)
    )

    table_loads = [
        pltpu.make_async_copy(table.at[k, 0], tables_in.at[i], load_sem.at[2 + i])
        for i, table in enumerate((segments, patch_rows, patch_cols))
    ]
    for copy in table_loads:
        copy.start()

    pl.semaphore_wait(barrier, expected)

    def rows_at(start, size):
        return pl.ds(pl.multiple_of(start, SHARD), size)

    full_in = (x1, g2)
    downs = (down_x, down_cot)
    ups = (up_x, up_cot)
    down_init = []
    up_init = []
    down_local = []
    for i in range(2):
        spot = full_in[i].at[0, rows_at(c * CHUNK + k * SHARD, SHARD), :]
        up_init.append(
            remote(
                ups[i],
                spot,
                init_send.at[i, 0],
                init_recv.at[i, k],
                (mirror, 2 * c + 1, d),
            )
        )
        down_init.append(
            remote(
                downs[i],
                spot,
                init_send.at[i, 1],
                init_recv.at[i, k],
                (p, 2 * c, d),
            )
        )
        down_local.append(
            pltpu.make_async_copy(
                downs[i], full_in[i].at[0, rows_at(c * CHUNK, SHARD), :], load_sem.at[5 + i]
            )
        )
    for i in range(2):
        up_init[i].start()

        @pl.when(k == 1)
        def _():
            down_init[i].start()

        @pl.when(k == 0)
        def _():
            down_local[i].start()

    swaps = [
        remote(w_qkv, wq.at[1], swap_send.at[0], swap_recv.at[0], core_mate),
        remote(w_out, wo.at[1], swap_send.at[1], swap_recv.at[1], core_mate),
    ]
    @pl.when(k == 1)
    def _():
        start(swaps)

    for copy in table_loads:
        copy.wait()
    for tick, index in enumerate((index1, index2)):
        for i in range(3):
            meta[0, tick, pl.ds(i, 1), :] = tables_in[i, pl.ds(index, 1), :]
        meta[0, tick, 3:8, :] = jnp.zeros((5, TOK), jnp.int32)
    meta_copy = remote(meta.at[0], meta.at[1], meta_send, meta_recv, peer(p, 1, 0))
    meta_copy.start()

    def await_init(i):
        def landing(shard):
            spot = full_in[i].at[0, rows_at(c * CHUNK + shard * SHARD, SHARD), :]
            remote(
                downs[0], spot, init_send.at[i, 0], init_recv.at[i, shard], core_mate
            ).wait_recv()

        @pl.when(k == 1)
        def _():
            landing(0)

        @pl.when(k == 0)
        def _():
            down_local[i].wait()

        landing(1)

    def chunk_of(buffer, rep, chip):
        return buffer.at[rep, rows_at(chip * CHUNK, CHUNK), :]

    def gather(n, source, buffer, phase, rep, with_self):
        return [
            remote(
                source,
                chunk_of(buffer, rep, c),
                ag_send.at[n, rep, m],
                ag_recv.at[n, rep, m],
                peer(phase, rep, m),
            )
            for m in (3, 2, 1, 0)
            if m or rep or with_self
        ]

    def await_gather(n, buffer, rep, with_self):
        for m in range(CHIPS):
            if m or rep or with_self:
                remote(
                    reduced.at[0],
                    chunk_of(buffer, rep, c ^ m),
                    ag_send.at[n, rep, m],
                    ag_recv.at[n, rep, m],
                    core_mate,
                ).wait_recv()

    def tables(tick, rep):
        n = 2 * tick + rep
        row = lax.broadcasted_iota(jnp.int32, (HD, TOK), 0)
        power = (row % QUARTER).astype(F32)
        frequency = jnp.exp(power * (-math.log(10000.0) / QUARTER))
        position = jnp.where(
            row < 2 * QUARTER,
            jnp.broadcast_to(meta[rep, tick, 1:2, :], (HD, TOK)),
            jnp.broadcast_to(meta[rep, tick, 2:3, :], (HD, TOK)),
        ).astype(F32)
        angle = position * frequency
        first = (row < QUARTER) | ((row >= 2 * QUARTER) & (row < 3 * QUARTER))
        cosine[n] = jnp.cos(angle)
        turned = jnp.sin(angle)
        sine[n] = jnp.where(first, -turned, turned)
        ids = jnp.broadcast_to(meta[rep, tick, 0:1, :].astype(F32), (TOK, TOK))
        mask[n] = jnp.where(ids == ids.T, 1.0, 0.0)

    def flip_weights(slot):
        small = identity(TOK)

        def body(j, _):
            at = pl.ds(pl.multiple_of(j * TOK, TOK), TOK)
            wq_t[slot, at, :] = dot_nt(small, wq[slot, :, at]).astype(BF16)
            wo_t[slot, at, :] = dot_nt(small, wo[slot, :, at]).astype(BF16)
            return 0

        lax.fori_loop(0, D // TOK, body, 0)

    scale = 1.0 / math.sqrt(HD)

    def forward_head(n, slot, head):
        at = head * HD
        yq, sq = normalize(project[slot, at : at + HD, :])
        yk, sk = normalize(project[slot, SHARD + at : SHARD + at + HD, :])
        v = project[slot, 2 * SHARD + at : 2 * SHARD + at + HD, :].astype(BF16)
        qr = (yq * cosine[n] + swap_pairs(yq) * sine[n]).astype(BF16)
        kr = (yk * cosine[n] + swap_pairs(yk) * sine[n]).astype(BF16)
        raised = jnp.where(mask[n] > 0.5, jnp.exp(dot_tn(kr, qr) * scale), 0.0)
        soft = raised / jnp.sum(raised, axis=0, keepdims=True)
        blended = dot_nn(v, soft.astype(BF16))
        return yq, sq, yk, sk, qr, kr, v, soft, blended.astype(BF16)

    def backward_head(n, state, grad):
        yq, sq, yk, sk, qr, kr, v, soft = state
        gb = grad.astype(BF16)
        d_soft = dot_tn(v, gb)
        mean = jnp.sum(soft * d_soft, axis=0, keepdims=True)
        d_score = (soft * (d_soft - mean)).astype(BF16)
        dv = dot_nt(gb, soft.astype(BF16))
        dq = dot_nn(kr, d_score) * scale
        dk = dot_nt(qr, d_score) * scale
        dq = dq * cosine[n] - swap_pairs(dq) * sine[n]
        dk = dk * cosine[n] - swap_pairs(dk) * sine[n]
        dq = pull_normalize(dq, yq, sq)
        dk = pull_normalize(dk, yk, sk)
        return dq.astype(BF16), dk.astype(BF16), dv.astype(BF16)

    def run_project(buffer, rep):
        x = buffer[rep]
        for slot in range(2):
            project[slot] = dot_nn(wq[slot], x)

    def run_grad_o(buffer, rep):
        g = buffer[rep]
        for slot in range(2):
            grad_o[slot] = dot_nn(wo[slot], g)

    def forward_first(rep):
        run_project(x1, rep)

        def body(slot, _):
            for head in range(2):
                yq, sq, yk, sk, qr, kr, v, soft, o = forward_head(rep, slot, head)
                ys[rep, slot, head, 0] = yq
                ys[rep, slot, head, 1] = yk
                scales[rep, slot, head, 0:1, :] = sq
                scales[rep, slot, head, 1:2, :] = sk
                qkv[rep, slot, head, 0] = qr
                qkv[rep, slot, head, 1] = kr
                qkv[rep, slot, head, 2] = v
                weights[rep, slot, head] = soft
                heads1[rep, slot, head * HD : (head + 1) * HD, :] = o
            return 0

        lax.fori_loop(0, 2, body, 0)

    def keep(buffer, rep, slot, head, grads):
        for i in range(3):
            at = i * SHARD + head * HD
            buffer[rep, slot, at : at + HD, :] = grads[i]

    def both_second(rep):
        run_project(x2, rep)

        def body(slot, _):
            for head in range(2):
                values = forward_head(2 + rep, slot, head)
                heads2[rep, slot, head * HD : (head + 1) * HD, :] = values[8]
                grad = grad_o[slot, head * HD : (head + 1) * HD, :]
                keep(dp2, rep, slot, head, backward_head(2 + rep, values[:8], grad))
            return 0

        lax.fori_loop(0, 2, body, 0)

    def backward_first(rep):
        def body(slot, _):
            for head in range(2):
                state = (
                    ys[rep, slot, head, 0],
                    scales[rep, slot, head, 0:1, :],
                    ys[rep, slot, head, 1],
                    scales[rep, slot, head, 1:2, :],
                    qkv[rep, slot, head, 0],
                    qkv[rep, slot, head, 1],
                    qkv[rep, slot, head, 2],
                    weights[rep, slot, head],
                )
                grad = grad_o[slot, head * HD : (head + 1) * HD, :]
                keep(dp1, rep, slot, head, backward_head(rep, state, grad))
            return 0

        lax.fori_loop(0, 2, body, 0)

    def send_partials(n, flipped, small):
        copies = []
        for m in (3, 2, 1, 0):
            at = rows_at((c ^ m) * CHUNK, CHUNK)
            total = dot_nn(flipped[0, at, :], small[0, 0]) + dot_nn(
                flipped[1, at, :], small[0, 1]
            )
            if m == 0:
                partial[n, 0] = total
            else:
                outgoing[n, m - 1] = total.astype(BF16)
                copies.append(
                    remote(
                        outgoing.at[n, m - 1],
                        landed.at[n, m - 1],
                        rs_send.at[n, m - 1],
                        rs_recv.at[n, m - 1],
                        peer(p, 0, m),
                    )
                )
                copies[-1].start()
        return copies

    def reduce_partials(n, copies, residual):
        total = residual[0, rows_at(c * CHUNK, CHUNK), :].astype(F32) + partial[n, 0]
        for copy in copies:
            copy.wait_recv()
        for m in range(1, CHIPS):
            total = total + landed[n, m - 1].astype(F32)
        reduced[n] = total.astype(BF16)

    half = 2 * CHUNK

    def relay(n, buffer):
        def piece(rep, start):
            return buffer.at[rep, pl.ds(start, half), :]

        def hand(start, chip, s):
            return remote(
                piece(0, start),
                piece(1, start),
                relay_send.at[n, s],
                relay_recv.at[n, 0],
                (p, 2 * chip + k, 1 - d),
            )

        first = [hand(0, 3, 0), hand(0, 1, 1)]
        last = [hand(half, 0, 0), hand(half, 2, 1)]
        mine = pl.multiple_of((1 - c % 2) * half, half)
        other = pl.multiple_of((c % 2) * half, half)
        onward = remote(
            piece(1, mine), piece(1, mine), relay_send.at[n, 2], relay_recv.at[n, 1], peer(p, 0, 1)
        )

        def begin():
            @pl.when(c == 0)
            def _():
                start(first)

            @pl.when(c == 3)
            def _():
                start(last)

        def forward():
            remote(
                piece(0, 0), piece(1, mine), relay_send.at[n, 0], relay_recv.at[n, 0], core_mate
            ).wait_recv()
            onward.start()

        def finish():
            remote(
                piece(0, 0), piece(1, other), relay_send.at[n, 0], relay_recv.at[n, 1], core_mate
            ).wait_recv()

        def drain():
            onward.wait_send()

            @pl.when(c == 0)
            def _():
                for copy in first:
                    copy.wait_send()

            @pl.when(c == 3)
            def _():
                for copy in last:
                    copy.wait_send()

        return begin, forward, finish, drain

    def direct(n, source, buffer, phase):
        chip = jnp.where(c >= 2, 0, 1)
        return [
            remote(
                source,
                chunk_of(buffer, 1, c),
                ag_send.at[n, 1, i],
                ag_recv.at[n, 1, c % 2],
                (phase, 2 * (chip + 2 * i) + k, 1 - d),
            )
            for i in range(2)
        ]

    def direct_relay(n, buffer):
        mine = pl.multiple_of((1 - c % 2) * half, half)
        other = pl.multiple_of((c % 2) * half, half)

        def piece(start):
            return buffer.at[1, pl.ds(start, half), :]

        onward = remote(
            piece(mine), piece(mine), relay_send.at[3, 2], relay_recv.at[3, 1], peer(p, 0, 1)
        )

        def forward():
            for i in range(2):
                remote(
                    reduced.at[0],
                    buffer.at[1, pl.ds(pl.multiple_of(mine + i * CHUNK, CHUNK), CHUNK), :],
                    ag_send.at[n, 1, i],
                    ag_recv.at[n, 1, i],
                    core_mate,
                ).wait_recv()
            onward.start()

        def finish():
            remote(
                piece(mine), piece(other), relay_send.at[3, 2], relay_recv.at[3, 1], core_mate
            ).wait_recv()

        return forward, finish, onward

    x1_relay = relay(0, x1)
    x2_relay = relay(1, x2)
    cot_relay = relay(2, g2)

    await_init(0)
    x1_own = gather(0, chunk_of(x1, 0, c), x1, p, 0, False)
    start(x1_own)

    @pl.when(k == 0)
    def _():
        start(swaps)

    tables(0, 0)
    for copy in loads:
        copy.wait()
    flip_weights(0)
    await_init(1)
    cot_own = gather(1, chunk_of(g2, 0, c), g2, p, 0, False)
    for copy in swaps:
        copy.wait_recv()
    flip_weights(1)
    await_gather(0, x1, 0, False)
    start(cot_own)
    forward_first(0)
    rs1 = send_partials(0, wo_t, heads1)
    tables(1, 0)
    meta_copy.wait_recv()
    tables(0, 1)
    tables(1, 1)
    reduce_partials(0, rs1, x1)

    x2_own = gather(2, reduced.at[0], x2, p + 1, 0, True)

    @pl.when(has_next)
    def _():
        start(x2_own)

    await_gather(1, g2, 0, False)
    run_grad_o(g2, 0)
    x1_relay[0]()
    cot_relay[0]()

    @pl.when(has_last)
    def _():
        await_gather(2, x2, 0, True)

    @pl.when(p == 0)
    def _():
        x2[0] = jnp.zeros_like(x2[0])

    both_second(0)
    rs2 = send_partials(1, wq_t, dp2)
    x2_relay[0]()
    x1_relay[1]()
    reduce_partials(1, rs2, g2)
    g1_own = gather(3, reduced.at[1], g1, p - 1, 0, True)
    g1_other = direct(3, reduced.at[1], g1, p - 1)
    g1_forward, g1_finish, g1_onward = direct_relay(3, g1)

    @pl.when(has_last)
    def _():
        start(g1_own)
        start(g1_other)

    cot_relay[1]()
    x1_relay[2]()
    forward_first(1)
    x2_relay[1]()

    def gradient(slot, j, tick):
        dps, xs = (dp1, x1) if tick == 0 else (dp2, x2)
        at = pl.ds(pl.multiple_of(j * SHARD, SHARD), SHARD)
        left = jnp.concatenate([dps[0, slot, at, :], dps[1, slot, at, :]], axis=1)
        right = jnp.concatenate([xs[0], xs[1]], axis=1)
        return dot_nt(left, right)

    def gradient_out(slot, tick):
        hs, gs = (heads1, g1) if tick == 0 else (heads2, g2)
        left = jnp.concatenate([hs[0, slot], hs[1, slot]], axis=1)
        right = jnp.concatenate([gs[0], gs[1]], axis=1)
        return dot_nt(left, right)

    def second_sums(i, _):
        slot = i // 3
        j = i % 3
        sums[slot, j] = gradient(slot, j, 1)
        return 0

    @pl.when(has_next)
    def _():
        await_gather(3, g1, 0, True)

    @pl.when(p == PHASES - 1)
    def _():
        g1[...] = jnp.zeros_like(g1)

    run_grad_o(g1, 0)
    backward_first(0)
    rs3 = send_partials(2, wq_t, dp1)

    @pl.when(has_next)
    def _():
        g1_forward()

    cot_relay[2]()
    run_grad_o(g2, 1)
    x2_relay[2]()
    both_second(1)
    lax.fori_loop(0, 6, second_sums, 0)
    for slot in range(2):
        sums[slot, 3] = gradient_out(slot, 1)
    reduce_partials(2, rs3, g1)

    up_fin = [
        remote(
            reduced.at[2, pl.ds(s * SHARD, SHARD), :],
            final.at[1],
            fin_send.at[s],
            fin_recv.at[1],
            (mirror, 2 * c + s, d),
        )
        for s in range(2)
    ]
    down_fin = remote(
        reduced.at[2, pl.ds(SHARD, SHARD), :], final.at[0], fin_send.at[0], fin_recv.at[0], core_mate
    )

    down_kept = pltpu.make_async_copy(
        reduced.at[2, pl.ds(0, SHARD), :], final.at[0], load_sem.at[7]
    )

    @pl.when(k == 1)
    def _():
        start(up_fin)

    @pl.when(k == 0)
    def _():
        down_fin.start()
        down_kept.start()

    @pl.when(has_next)
    def _():
        g1_finish()

    run_grad_o(g1, 1)
    backward_first(1)

    handed = [
        remote(sums_in.at[0, j], sums_in.at[1, j], gw_send.at[j], gw_recv.at[j], core_mate)
        for j in range(4)
    ]
    for j in range(4):
        more = gradient(1, j, 0) if j < 3 else gradient_out(1, 0)
        sums_in[0, j] = (sums[1, j] + more).astype(BF16)
        handed[j].start()
    results = []
    for j in range(4):
        more = gradient(0, j, 0) if j < 3 else gradient_out(0, 0)
        total = sums[0, j] + more
        handed[j].wait_recv()
        sums_in[2, j] = (total + sums_in[1, j].astype(F32)).astype(BF16)
        target = out_qkv.at[pl.ds(j * SHARD, SHARD), :] if j < 3 else out_wo
        results.append(pltpu.make_async_copy(sums_in.at[2, j], target, out_sem.at[j]))
        results[-1].start()

    @pl.when(k == 1)
    def _():
        remote(downs[0], final.at[0], fin_send.at[0], fin_recv.at[0], core_mate).wait_recv()

    @pl.when(k == 0)
    def _():
        down_kept.wait()

    remote(downs[0], final.at[1], fin_send.at[0], fin_recv.at[1], core_mate).wait_recv()
    for i, target in enumerate((out_down, out_up)):
        results.append(pltpu.make_async_copy(final.at[i], target, out_sem.at[4 + i]))
        results[-1].start()

    for copy in up_init + swaps + [meta_copy] + x1_own + cot_own:
        copy.wait_send()
    for line in (x1_relay, x2_relay, cot_relay):
        line[3]()
    for copy in rs1 + rs2 + rs3 + handed:
        copy.wait_send()

    @pl.when(k == 1)
    def _():
        for copy in down_init + up_fin:
            copy.wait_send()

    @pl.when(k == 0)
    def _():
        down_fin.wait_send()

    @pl.when(has_next)
    def _():
        for copy in x2_own:
            copy.wait_send()

    @pl.when(has_last)
    def _():
        for copy in g1_own + g1_other:
            copy.wait_send()

    @pl.when(has_next)
    def _():
        g1_onward.wait_send()

    for copy in results:
        copy.wait()


def place(*refs):
    sources, targets, kept, sem = refs[:4], refs[4:8], refs[8:12], refs[12]
    pieces = []
    for i, count in enumerate((1, 1, 6, 2)):
        rows = sources[i].shape[0] // count
        pieces += [(i, pl.ds(j * rows, rows)) for j in range(count)]
    inward = [
        pltpu.make_async_copy(sources[i].at[at], kept[i].at[at], sem.at[0, n])
        for n, (i, at) in enumerate(pieces)
    ]
    outward = [
        pltpu.make_async_copy(kept[i].at[at], targets[i].at[at], sem.at[1, n])
        for n, (i, at) in enumerate(pieces)
    ]
    for copy in inward:
        copy.start()
    for before, copy in zip(inward, outward):
        before.wait()
        copy.start()
    for copy in outward:
        copy.wait()


def per_device(
    down_inputs, up_inputs, down_cot, up_cot, segment_ids, patch_rows, patch_cols, w_qkv, w_out
):
    hbm = pl.BlockSpec(memory_space=pltpu.HBM)
    dma = pltpu.SemaphoreType.DMA
    tok_block = jax.ShapeDtypeStruct((SHARD, TOK), BF16)
    shapes = (
        tok_block,
        tok_block,
        jax.ShapeDtypeStruct((ROWS, D), BF16),
        jax.ShapeDtypeStruct((SHARD, D), BF16),
    )
    outs = pl.pallas_call(
        kernel,
        out_shape=shapes,
        in_specs=[hbm] * 9,
        out_specs=(hbm,) * 4,
        scratch_shapes=[
            pltpu.VMEM((3, PHASES, TOK), jnp.int32),
            pltpu.VMEM((2, 2, 8, TOK), jnp.int32),
            pltpu.VMEM((4, HD, TOK), F32),
            pltpu.VMEM((4, HD, TOK), F32),
            pltpu.VMEM((4, TOK, TOK), F32),
            pltpu.VMEM((2, ROWS, D), BF16),
            pltpu.VMEM((2, SHARD, D), BF16),
            pltpu.VMEM((2, D, ROWS), BF16),
            pltpu.VMEM((2, D, SHARD), BF16),
            pltpu.VMEM((2, D, TOK), BF16),
            pltpu.VMEM((2, D, TOK), BF16),
            pltpu.VMEM((2, D, TOK), BF16),
            pltpu.VMEM((2, D, TOK), BF16),
            pltpu.VMEM((2, ROWS, TOK), F32),
            pltpu.VMEM((2, SHARD, TOK), F32),
            pltpu.VMEM((2, 2, 2, 2, HD, TOK), F32),
            pltpu.VMEM((2, 2, 2, 8, TOK), F32),
            pltpu.VMEM((2, 2, 2, 3, HD, TOK), BF16),
            pltpu.VMEM((2, 2, 2, TOK, TOK), F32),
            pltpu.VMEM((2, 2, SHARD, TOK), BF16),
            pltpu.VMEM((2, 2, SHARD, TOK), BF16),
            pltpu.VMEM((2, 2, ROWS, TOK), BF16),
            pltpu.VMEM((2, 2, ROWS, TOK), BF16),
            pltpu.VMEM((3, 1, CHUNK, TOK), F32),
            pltpu.VMEM((3, 3, CHUNK, TOK), BF16),
            pltpu.VMEM((3, CHUNK, TOK), BF16),
            pltpu.VMEM((2, SHARD, TOK), BF16),
            pltpu.VMEM((2, 4, SHARD, D), F32),
            pltpu.VMEM((3, 4, SHARD, D), BF16),
            pltpu.VMEM((3, 3, CHUNK, TOK), BF16),
            dma((8,)),
            dma((2,)),
            dma((2,)),
            dma((2, 2)),
            dma((2, 2)),
            dma,
            dma,
            dma((4, 2, 4)),
            dma((4, 2, 4)),
            dma((4, 3)),
            dma((4, 2)),
            dma((3, 3)),
            dma((3, 3)),
            dma((2,)),
            dma((2,)),
            dma((4,)),
            dma((4,)),
            dma((6,)),
        ],
        compiler_params=pltpu.CompilerParams(
            collective_id=0, has_side_effects=True, vmem_limit_bytes=60 << 20
        ),
    )(
        down_inputs[0, 0].T,
        up_inputs[0, 0].T,
        down_cot[0, 0].T,
        up_cot[0, 0].T,
        segment_ids,
        patch_rows,
        patch_cols,
        w_qkv.reshape(ROWS, D),
        w_out[0],
    )
    outs = pl.pallas_call(
        place,
        out_shape=shapes,
        in_specs=[hbm] * 4,
        out_specs=(hbm,) * 4,
        scratch_shapes=[pltpu.VMEM(x.shape, BF16) for x in shapes] + [dma((2, 10))],
        compiler_params=pltpu.CompilerParams(vmem_limit_bytes=60 << 20),
    )(*outs)
    return (
        outs[0].T[None, None],
        outs[1].T[None, None],
        outs[2].reshape(w_qkv.shape),
        outs[3][None],
    )


def solution(mesh):
    return jax.shard_map(
        per_device,
        mesh=mesh,
        in_specs=(
            P("dp", "phase", None, "tp"),
            P("dp", "phase", None, "tp"),
            P("dp", "phase", None, "tp"),
            P("dp", "phase", None, "tp"),
            P(None, "dp", None, None),
            P(None, "dp", None, None),
            P(None, "dp", None, None),
            P("phase", None, "tp", None),
            P("phase", "tp", None),
        ),
        out_specs=(
            P("dp", "phase", None, "tp"),
            P("dp", "phase", None, "tp"),
            P("phase", None, "tp", None),
            P("phase", "tp", None),
        ),
        check_vma=False,
    )
```

```python
import functools
import math

import jax
import jax.numpy as jnp
from jax import lax
from jax.experimental import pallas as pl
from jax.experimental.pallas import tpu as pltpu
from jax.sharding import PartitionSpec as P

HD = 80
QUARTER = 20
TOK = 128
D = 1280
SHARD = 160
CHUNK = 320
CHIPS = 4
HEADS = 4
PHASES = 32
ROWS = 480
MESH = pl.DeviceIdType.MESH
F32 = jnp.float32
BF16 = jnp.bfloat16


def dot_nn(a, b):
    return lax.dot_general(a, b, (((1,), (0,)), ((), ())), preferred_element_type=F32)


def dot_nt(a, b):
    return lax.dot_general(a, b, (((1,), (1,)), ((), ())), preferred_element_type=F32)


def dot_tn(a, b):
    return lax.dot_general(a, b, (((0,), (0,)), ((), ())), preferred_element_type=F32)


def normalize(x):
    centred = x - jnp.mean(x, axis=0, keepdims=True)
    scale = lax.rsqrt(jnp.mean(centred * centred, axis=0, keepdims=True) + 1e-06)
    return centred * scale, scale


def pull_normalize(grad, y, scale):
    return scale * (
        grad
        - jnp.mean(grad, axis=0, keepdims=True)
        - y * jnp.mean(grad * y, axis=0, keepdims=True)
    )


def swap_pairs(y):
    row = lax.broadcasted_iota(jnp.int32, y.shape, 0)
    first = (row < QUARTER) | ((row >= 2 * QUARTER) & (row < 3 * QUARTER))
    return jnp.where(first, pltpu.roll(y, HD - QUARTER, axis=0), pltpu.roll(y, QUARTER, axis=0))


def identity(size):
    row = lax.broadcasted_iota(jnp.int32, (size, size), 0)
    column = lax.broadcasted_iota(jnp.int32, (size, size), 1)
    return jnp.where(row == column, 1.0, 0.0).astype(BF16)


def kernel(
    down_x,
    up_x,
    down_cot,
    up_cot,
    segments,
    patch_rows,
    patch_cols,
    w_qkv,
    w_out,
    out_down,
    out_up,
    out_qkv,
    out_wo,
    tables_in,
    meta,
    cosine,
    sine,
    mask,
    wq,
    wo,
    wq_t,
    wo_t,
    x1,
    x2,
    g1,
    g2,
    project,
    grad_o,
    ys,
    scales,
    qkv,
    weights,
    heads1,
    heads2,
    dp1,
    dp2,
    partial,
    landed,
    reduced,
    final,
    sums,
    sums_in,
    outgoing,
    load_sem,
    swap_send,
    swap_recv,
    init_send,
    init_recv,
    meta_send,
    meta_recv,
    ag_send,
    ag_recv,
    relay_send,
    relay_recv,
    rs_send,
    rs_recv,
    fin_send,
    fin_recv,
    gw_send,
    gw_recv,
    out_sem,
):
    p = lax.axis_index("phase")
    tp = lax.axis_index("tp")
    d = lax.axis_index("dp")
    c = tp // 2
    k = tp % 2
    mirror = PHASES - 1 - p
    has_next = p < PHASES - 1
    has_last = p > 0
    index1 = jnp.where(k == 0, p, mirror)
    back = jnp.maximum(p - 1, 0)
    index2 = jnp.where(k == 0, back, PHASES - 1 - back)

    def remote(src, dst, send, recv, device):
        return pltpu.make_async_remote_copy(
            src_ref=src,
            dst_ref=dst,
            send_sem=send,
            recv_sem=recv,
            device_id=device,
            device_id_type=MESH,
        )

    def peer(phase, rep, m):
        other = 2 * (c ^ m) + k
        return (phase, other, d if rep == 0 else 1 - d)

    core_mate = (p, 2 * c + 1 - k, d)

    def start(copies):
        for copy in copies:
            copy.start()

    loads = [
        pltpu.make_async_copy(w_qkv, wq.at[0], load_sem.at[0]),
        pltpu.make_async_copy(w_out, wo.at[0], load_sem.at[1]),
    ]
    for copy in loads:
        copy.start()

    barrier = pltpu.get_barrier_semaphore()

    def greet(device):
        pl.semaphore_signal(barrier, inc=1, device_id=device, device_id_type=MESH)

    greet(core_mate)
    for m in range(1, CHIPS):
        greet(peer(p, 0, m))
    for m in range(CHIPS):
        greet(peer(p, 1, m))
    greet((mirror, 2 * c + 1, d))

    @pl.when(k == 1)
    def _():
        greet((mirror, 2 * c, d))

    @pl.when(has_last)
    def _():
        for m in range(CHIPS):
            greet(peer(p - 1, 0, m))

    @pl.when(has_next)
    def _():
        for rep in range(2):
            for m in range(CHIPS):
                greet(peer(p + 1, rep, m))

    expected = (
        8
        + 1
        + k
        + 4 * jnp.where(has_next, 1, 0)
        + 8 * jnp.where(has_last, 1, 0)
    )

    table_loads = [
        pltpu.make_async_copy(table.at[k, 0], tables_in.at[i], load_sem.at[2 + i])
        for i, table in enumerate((segments, patch_rows, patch_cols))
    ]
    for copy in table_loads:
        copy.start()

    pl.semaphore_wait(barrier, expected)

    def rows_at(start, size):
        return pl.ds(pl.multiple_of(start, SHARD), size)

    full_in = (x1, g2)
    downs = (down_x, down_cot)
    ups = (up_x, up_cot)
    down_init = []
    up_init = []
    down_local = []
    for i in range(2):
        spot = full_in[i].at[0, rows_at(c * CHUNK + k * SHARD, SHARD), :]
        up_init.append(
            remote(
                ups[i],
                spot,
                init_send.at[i, 0],
                init_recv.at[i, k],
                (mirror, 2 * c + 1, d),
            )
        )
        down_init.append(
            remote(
                downs[i],
                spot,
                init_send.at[i, 1],
                init_recv.at[i, k],
                (p, 2 * c, d),
            )
        )
        down_local.append(
            pltpu.make_async_copy(
                downs[i], full_in[i].at[0, rows_at(c * CHUNK, SHARD), :], load_sem.at[5 + i]
            )
        )
    for i in range(2):
        up_init[i].start()

        @pl.when(k == 1)
        def _():
            down_init[i].start()

        @pl.when(k == 0)
        def _():
            down_local[i].start()

    swaps = [
        remote(w_qkv, wq.at[1], swap_send.at[0], swap_recv.at[0], core_mate),
        remote(w_out, wo.at[1], swap_send.at[1], swap_recv.at[1], core_mate),
    ]
    @pl.when(k == 1)
    def _():
        start(swaps)

    for copy in table_loads:
        copy.wait()
    for tick, index in enumerate((index1, index2)):
        for i in range(3):
            meta[0, tick, pl.ds(i, 1), :] = tables_in[i, pl.ds(index, 1), :]
        meta[0, tick, 3:8, :] = jnp.zeros((5, TOK), jnp.int32)
    meta_copy = remote(meta.at[0], meta.at[1], meta_send, meta_recv, peer(p, 1, 0))
    meta_copy.start()

    def await_init(i):
        def landing(shard):
            spot = full_in[i].at[0, rows_at(c * CHUNK + shard * SHARD, SHARD), :]
            remote(
                downs[0], spot, init_send.at[i, 0], init_recv.at[i, shard], core_mate
            ).wait_recv()

        @pl.when(k == 1)
        def _():
            landing(0)

        @pl.when(k == 0)
        def _():
            down_local[i].wait()

        landing(1)

    def chunk_of(buffer, rep, chip):
        return buffer.at[rep, rows_at(chip * CHUNK, CHUNK), :]

    def gather(n, source, buffer, phase, rep, with_self):
        return [
            remote(
                source,
                chunk_of(buffer, rep, c),
                ag_send.at[n, rep, m],
                ag_recv.at[n, rep, m],
                peer(phase, rep, m),
            )
            for m in (3, 2, 1, 0)
            if m or rep or with_self
        ]

    def await_gather(n, buffer, rep, with_self):
        for m in range(CHIPS):
            if m or rep or with_self:
                remote(
                    reduced.at[0],
                    chunk_of(buffer, rep, c ^ m),
                    ag_send.at[n, rep, m],
                    ag_recv.at[n, rep, m],
                    core_mate,
                ).wait_recv()

    def tables(tick, rep):
        n = 2 * tick + rep
        row = lax.broadcasted_iota(jnp.int32, (HD, TOK), 0)
        power = (row % QUARTER).astype(F32)
        frequency = jnp.exp(power * (-math.log(10000.0) / QUARTER))
        position = jnp.where(
            row < 2 * QUARTER,
            jnp.broadcast_to(meta[rep, tick, 1:2, :], (HD, TOK)),
            jnp.broadcast_to(meta[rep, tick, 2:3, :], (HD, TOK)),
        ).astype(F32)
        angle = position * frequency
        first = (row < QUARTER) | ((row >= 2 * QUARTER) & (row < 3 * QUARTER))
        cosine[n] = jnp.cos(angle)
        turned = jnp.sin(angle)
        sine[n] = jnp.where(first, -turned, turned)
        ids = jnp.broadcast_to(meta[rep, tick, 0:1, :].astype(F32), (TOK, TOK))
        mask[n] = jnp.where(ids == ids.T, 1.0, 0.0)

    def flip_weights(slot):
        small = identity(TOK)

        def body(j, _):
            at = pl.ds(pl.multiple_of(j * TOK, TOK), TOK)
            wq_t[slot, at, :] = dot_nt(small, wq[slot, :, at]).astype(BF16)
            wo_t[slot, at, :] = dot_nt(small, wo[slot, :, at]).astype(BF16)
            return 0

        lax.fori_loop(0, D // TOK, body, 0)

    scale = 1.0 / math.sqrt(HD)

    def forward_head(n, slot, head):
        at = head * HD
        yq, sq = normalize(project[slot, at : at + HD, :])
        yk, sk = normalize(project[slot, SHARD + at : SHARD + at + HD, :])
        v = project[slot, 2 * SHARD + at : 2 * SHARD + at + HD, :].astype(BF16)
        qr = (yq * cosine[n] + swap_pairs(yq) * sine[n]).astype(BF16)
        kr = (yk * cosine[n] + swap_pairs(yk) * sine[n]).astype(BF16)
        raised = jnp.where(mask[n] > 0.5, jnp.exp(dot_tn(kr, qr) * scale), 0.0)
        soft = raised / jnp.sum(raised, axis=0, keepdims=True)
        blended = dot_nn(v, soft.astype(BF16))
        return yq, sq, yk, sk, qr, kr, v, soft, blended.astype(BF16)

    def backward_head(n, state, grad):
        yq, sq, yk, sk, qr, kr, v, soft = state
        gb = grad.astype(BF16)
        d_soft = dot_tn(v, gb)
        mean = jnp.sum(soft * d_soft, axis=0, keepdims=True)
        d_score = (soft * (d_soft - mean)).astype(BF16)
        dv = dot_nt(gb, soft.astype(BF16))
        dq = dot_nn(kr, d_score) * scale
        dk = dot_nt(qr, d_score) * scale
        dq = dq * cosine[n] - swap_pairs(dq) * sine[n]
        dk = dk * cosine[n] - swap_pairs(dk) * sine[n]
        dq = pull_normalize(dq, yq, sq)
        dk = pull_normalize(dk, yk, sk)
        return dq.astype(BF16), dk.astype(BF16), dv.astype(BF16)

    def run_project(buffer, rep):
        x = buffer[rep]
        for slot in range(2):
            project[slot] = dot_nn(wq[slot], x)

    def run_grad_o(buffer, rep):
        g = buffer[rep]
        for slot in range(2):
            grad_o[slot] = dot_nn(wo[slot], g)

    def forward_first(rep):
        run_project(x1, rep)

        def body(slot, _):
            for head in range(2):
                yq, sq, yk, sk, qr, kr, v, soft, o = forward_head(rep, slot, head)
                ys[rep, slot, head, 0] = yq
                ys[rep, slot, head, 1] = yk
                scales[rep, slot, head, 0:1, :] = sq
                scales[rep, slot, head, 1:2, :] = sk
                qkv[rep, slot, head, 0] = qr
                qkv[rep, slot, head, 1] = kr
                qkv[rep, slot, head, 2] = v
                weights[rep, slot, head] = soft
                heads1[rep, slot, head * HD : (head + 1) * HD, :] = o
            return 0

        lax.fori_loop(0, 2, body, 0)

    def keep(buffer, rep, slot, head, grads):
        for i in range(3):
            at = i * SHARD + head * HD
            buffer[rep, slot, at : at + HD, :] = grads[i]

    def both_second(rep):
        run_project(x2, rep)

        def body(slot, _):
            for head in range(2):
                values = forward_head(2 + rep, slot, head)
                heads2[rep, slot, head * HD : (head + 1) * HD, :] = values[8]
                grad = grad_o[slot, head * HD : (head + 1) * HD, :]
                keep(dp2, rep, slot, head, backward_head(2 + rep, values[:8], grad))
            return 0

        lax.fori_loop(0, 2, body, 0)

    def backward_first(rep):
        def body(slot, _):
            for head in range(2):
                state = (
                    ys[rep, slot, head, 0],
                    scales[rep, slot, head, 0:1, :],
                    ys[rep, slot, head, 1],
                    scales[rep, slot, head, 1:2, :],
                    qkv[rep, slot, head, 0],
                    qkv[rep, slot, head, 1],
                    qkv[rep, slot, head, 2],
                    weights[rep, slot, head],
                )
                grad = grad_o[slot, head * HD : (head + 1) * HD, :]
                keep(dp1, rep, slot, head, backward_head(rep, state, grad))
            return 0

        lax.fori_loop(0, 2, body, 0)

    def send_partials(n, flipped, small):
        copies = []
        for m in (3, 2, 1, 0):
            at = rows_at((c ^ m) * CHUNK, CHUNK)
            total = dot_nn(flipped[0, at, :], small[0, 0]) + dot_nn(
                flipped[1, at, :], small[0, 1]
            )
            if m == 0:
                partial[n, 0] = total
            else:
                outgoing[n, m - 1] = total.astype(BF16)
                copies.append(
                    remote(
                        outgoing.at[n, m - 1],
                        landed.at[n, m - 1],
                        rs_send.at[n, m - 1],
                        rs_recv.at[n, m - 1],
                        peer(p, 0, m),
                    )
                )
                copies[-1].start()
        return copies

    def reduce_partials(n, copies, residual):
        total = residual[0, rows_at(c * CHUNK, CHUNK), :].astype(F32) + partial[n, 0]
        for copy in copies:
            copy.wait_recv()
        for m in range(1, CHIPS):
            total = total + landed[n, m - 1].astype(F32)
        reduced[n] = total.astype(BF16)

    half = 2 * CHUNK

    def relay(n, buffer):
        def piece(rep, start):
            return buffer.at[rep, pl.ds(start, half), :]

        def hand(start, chip, s):
            return remote(
                piece(0, start),
                piece(1, start),
                relay_send.at[n, s],
                relay_recv.at[n, 0],
                (p, 2 * chip + k, 1 - d),
            )

        first = [hand(0, 3, 0), hand(0, 1, 1)]
        last = [hand(half, 0, 0), hand(half, 2, 1)]
        mine = pl.multiple_of((1 - c % 2) * half, half)
        other = pl.multiple_of((c % 2) * half, half)
        onward = remote(
            piece(1, mine), piece(1, mine), relay_send.at[n, 2], relay_recv.at[n, 1], peer(p, 0, 1)
        )

        def begin():
            @pl.when(c == 0)
            def _():
                start(first)

            @pl.when(c == 3)
            def _():
                start(last)

        def forward():
            remote(
                piece(0, 0), piece(1, mine), relay_send.at[n, 0], relay_recv.at[n, 0], core_mate
            ).wait_recv()
            onward.start()

        def finish():
            remote(
                piece(0, 0), piece(1, other), relay_send.at[n, 0], relay_recv.at[n, 1], core_mate
            ).wait_recv()

        def drain():
            onward.wait_send()

            @pl.when(c == 0)
            def _():
                for copy in first:
                    copy.wait_send()

            @pl.when(c == 3)
            def _():
                for copy in last:
                    copy.wait_send()

        return begin, forward, finish, drain

    def direct(n, source, buffer, phase):
        chip = jnp.where(c >= 2, 0, 1)
        return [
            remote(
                source,
                chunk_of(buffer, 1, c),
                ag_send.at[n, 1, i],
                ag_recv.at[n, 1, c % 2],
                (phase, 2 * (chip + 2 * i) + k, 1 - d),
            )
            for i in range(2)
        ]

    def direct_relay(n, buffer):
        mine = pl.multiple_of((1 - c % 2) * half, half)
        other = pl.multiple_of((c % 2) * half, half)

        def piece(start):
            return buffer.at[1, pl.ds(start, half), :]

        onward = remote(
            piece(mine), piece(mine), relay_send.at[3, 2], relay_recv.at[3, 1], peer(p, 0, 1)
        )

        def forward():
            for i in range(2):
                remote(
                    reduced.at[0],
                    buffer.at[1, pl.ds(pl.multiple_of(mine + i * CHUNK, CHUNK), CHUNK), :],
                    ag_send.at[n, 1, i],
                    ag_recv.at[n, 1, i],
                    core_mate,
                ).wait_recv()
            onward.start()

        def finish():
            remote(
                piece(mine), piece(other), relay_send.at[3, 2], relay_recv.at[3, 1], core_mate
            ).wait_recv()

        return forward, finish, onward

    x1_relay = relay(0, x1)
    x2_relay = relay(1, x2)
    cot_relay = relay(2, g2)

    await_init(0)
    x1_own = gather(0, chunk_of(x1, 0, c), x1, p, 0, False)
    start(x1_own)

    @pl.when(k == 0)
    def _():
        start(swaps)

    tables(0, 0)
    for copy in loads:
        copy.wait()
    flip_weights(0)
    await_init(1)
    cot_own = gather(1, chunk_of(g2, 0, c), g2, p, 0, False)
    for copy in swaps:
        copy.wait_recv()
    flip_weights(1)
    await_gather(0, x1, 0, False)
    start(cot_own)
    forward_first(0)
    rs1 = send_partials(0, wo_t, heads1)
    tables(1, 0)
    meta_copy.wait_recv()
    tables(0, 1)
    tables(1, 1)
    reduce_partials(0, rs1, x1)

    x2_own = gather(2, reduced.at[0], x2, p + 1, 0, True)

    @pl.when(has_next)
    def _():
        start(x2_own)

    await_gather(1, g2, 0, False)
    run_grad_o(g2, 0)
    x1_relay[0]()
    cot_relay[0]()

    @pl.when(has_last)
    def _():
        await_gather(2, x2, 0, True)

    @pl.when(p == 0)
    def _():
        x2[0] = jnp.zeros_like(x2[0])

    both_second(0)
    rs2 = send_partials(1, wq_t, dp2)
    x2_relay[0]()
    x1_relay[1]()
    reduce_partials(1, rs2, g2)
    g1_own = gather(3, reduced.at[1], g1, p - 1, 0, True)
    g1_other = direct(3, reduced.at[1], g1, p - 1)
    g1_forward, g1_finish, g1_onward = direct_relay(3, g1)

    @pl.when(has_last)
    def _():
        start(g1_own)
        start(g1_other)

    cot_relay[1]()
    x1_relay[2]()
    forward_first(1)
    x2_relay[1]()

    def gradient(slot, j, tick):
        dps, xs = (dp1, x1) if tick == 0 else (dp2, x2)
        at = pl.ds(pl.multiple_of(j * SHARD, SHARD), SHARD)
        left = jnp.concatenate([dps[0, slot, at, :], dps[1, slot, at, :]], axis=1)
        right = jnp.concatenate([xs[0], xs[1]], axis=1)
        return dot_nt(left, right)

    def gradient_out(slot, tick):
        hs, gs = (heads1, g1) if tick == 0 else (heads2, g2)
        left = jnp.concatenate([hs[0, slot], hs[1, slot]], axis=1)
        right = jnp.concatenate([gs[0], gs[1]], axis=1)
        return dot_nt(left, right)

    def second_sums(i, _):
        slot = i // 3
        j = i % 3
        sums[slot, j] = gradient(slot, j, 1)
        return 0

    @pl.when(has_next)
    def _():
        await_gather(3, g1, 0, True)

    @pl.when(p == PHASES - 1)
    def _():
        g1[...] = jnp.zeros_like(g1)

    @pl.when(has_next)
    def _():
        g1_forward()

    run_grad_o(g1, 0)
    backward_first(0)
    rs3 = send_partials(2, wq_t, dp1)

    cot_relay[2]()
    run_grad_o(g2, 1)
    x2_relay[2]()
    both_second(1)
    lax.fori_loop(0, 6, second_sums, 0)
    for slot in range(2):
        sums[slot, 3] = gradient_out(slot, 1)
    reduce_partials(2, rs3, g1)

    up_fin = [
        remote(
            reduced.at[2, pl.ds(s * SHARD, SHARD), :],
            final.at[1],
            fin_send.at[s],
            fin_recv.at[1],
            (mirror, 2 * c + s, d),
        )
        for s in range(2)
    ]
    down_fin = remote(
        reduced.at[2, pl.ds(SHARD, SHARD), :], final.at[0], fin_send.at[0], fin_recv.at[0], core_mate
    )

    down_kept = pltpu.make_async_copy(
        reduced.at[2, pl.ds(0, SHARD), :], final.at[0], load_sem.at[7]
    )

    @pl.when(k == 1)
    def _():
        start(up_fin)

    @pl.when(k == 0)
    def _():
        down_fin.start()
        down_kept.start()

    @pl.when(has_next)
    def _():
        g1_finish()

    run_grad_o(g1, 1)
    backward_first(1)

    handed = [
        remote(sums_in.at[0, j], sums_in.at[1, j], gw_send.at[j], gw_recv.at[j], core_mate)
        for j in range(4)
    ]
    for j in range(4):
        more = gradient(1, j, 0) if j < 3 else gradient_out(1, 0)
        sums_in[0, j] = (sums[1, j] + more).astype(BF16)
        handed[j].start()
    results = []
    for j in range(4):
        more = gradient(0, j, 0) if j < 3 else gradient_out(0, 0)
        total = sums[0, j] + more
        handed[j].wait_recv()
        sums_in[2, j] = (total + sums_in[1, j].astype(F32)).astype(BF16)
        target = out_qkv.at[pl.ds(j * SHARD, SHARD), :] if j < 3 else out_wo
        results.append(pltpu.make_async_copy(sums_in.at[2, j], target, out_sem.at[j]))
        results[-1].start()

    @pl.when(k == 1)
    def _():
        remote(downs[0], final.at[0], fin_send.at[0], fin_recv.at[0], core_mate).wait_recv()

    @pl.when(k == 0)
    def _():
        down_kept.wait()

    remote(downs[0], final.at[1], fin_send.at[0], fin_recv.at[1], core_mate).wait_recv()
    for i, target in enumerate((out_down, out_up)):
        results.append(pltpu.make_async_copy(final.at[i], target, out_sem.at[4 + i]))
        results[-1].start()

    for copy in up_init + swaps + [meta_copy] + x1_own + cot_own:
        copy.wait_send()
    for line in (x1_relay, x2_relay, cot_relay):
        line[3]()
    for copy in rs1 + rs2 + rs3 + handed:
        copy.wait_send()

    @pl.when(k == 1)
    def _():
        for copy in down_init + up_fin:
            copy.wait_send()

    @pl.when(k == 0)
    def _():
        down_fin.wait_send()

    @pl.when(has_next)
    def _():
        for copy in x2_own:
            copy.wait_send()

    @pl.when(has_last)
    def _():
        for copy in g1_own + g1_other:
            copy.wait_send()

    @pl.when(has_next)
    def _():
        g1_onward.wait_send()

    for copy in results:
        copy.wait()


def place(*refs):
    sources, targets, kept, sem = refs[:4], refs[4:8], refs[8:12], refs[12]
    pieces = []
    for i, count in enumerate((1, 1, 6, 2)):
        rows = sources[i].shape[0] // count
        pieces += [(i, pl.ds(j * rows, rows)) for j in range(count)]
    inward = [
        pltpu.make_async_copy(sources[i].at[at], kept[i].at[at], sem.at[0, n])
        for n, (i, at) in enumerate(pieces)
    ]
    outward = [
        pltpu.make_async_copy(kept[i].at[at], targets[i].at[at], sem.at[1, n])
        for n, (i, at) in enumerate(pieces)
    ]
    for copy in inward:
        copy.start()
    for before, copy in zip(inward, outward):
        before.wait()
        copy.start()
    for copy in outward:
        copy.wait()


def per_device(
    down_inputs, up_inputs, down_cot, up_cot, segment_ids, patch_rows, patch_cols, w_qkv, w_out
):
    hbm = pl.BlockSpec(memory_space=pltpu.HBM)
    dma = pltpu.SemaphoreType.DMA
    tok_block = jax.ShapeDtypeStruct((SHARD, TOK), BF16)
    shapes = (
        tok_block,
        tok_block,
        jax.ShapeDtypeStruct((ROWS, D), BF16),
        jax.ShapeDtypeStruct((SHARD, D), BF16),
    )
    outs = pl.pallas_call(
        kernel,
        out_shape=shapes,
        in_specs=[hbm] * 9,
        out_specs=(hbm,) * 4,
        scratch_shapes=[
            pltpu.VMEM((3, PHASES, TOK), jnp.int32),
            pltpu.VMEM((2, 2, 8, TOK), jnp.int32),
            pltpu.VMEM((4, HD, TOK), F32),
            pltpu.VMEM((4, HD, TOK), F32),
            pltpu.VMEM((4, TOK, TOK), F32),
            pltpu.VMEM((2, ROWS, D), BF16),
            pltpu.VMEM((2, SHARD, D), BF16),
            pltpu.VMEM((2, D, ROWS), BF16),
            pltpu.VMEM((2, D, SHARD), BF16),
            pltpu.VMEM((2, D, TOK), BF16),
            pltpu.VMEM((2, D, TOK), BF16),
            pltpu.VMEM((2, D, TOK), BF16),
            pltpu.VMEM((2, D, TOK), BF16),
            pltpu.VMEM((2, ROWS, TOK), F32),
            pltpu.VMEM((2, SHARD, TOK), F32),
            pltpu.VMEM((2, 2, 2, 2, HD, TOK), F32),
            pltpu.VMEM((2, 2, 2, 8, TOK), F32),
            pltpu.VMEM((2, 2, 2, 3, HD, TOK), BF16),
            pltpu.VMEM((2, 2, 2, TOK, TOK), F32),
            pltpu.VMEM((2, 2, SHARD, TOK), BF16),
            pltpu.VMEM((2, 2, SHARD, TOK), BF16),
            pltpu.VMEM((2, 2, ROWS, TOK), BF16),
            pltpu.VMEM((2, 2, ROWS, TOK), BF16),
            pltpu.VMEM((3, 1, CHUNK, TOK), F32),
            pltpu.VMEM((3, 3, CHUNK, TOK), BF16),
            pltpu.VMEM((3, CHUNK, TOK), BF16),
            pltpu.VMEM((2, SHARD, TOK), BF16),
            pltpu.VMEM((2, 4, SHARD, D), F32),
            pltpu.VMEM((3, 4, SHARD, D), BF16),
            pltpu.VMEM((3, 3, CHUNK, TOK), BF16),
            dma((8,)),
            dma((2,)),
            dma((2,)),
            dma((2, 2)),
            dma((2, 2)),
            dma,
            dma,
            dma((4, 2, 4)),
            dma((4, 2, 4)),
            dma((4, 3)),
            dma((4, 2)),
            dma((3, 3)),
            dma((3, 3)),
            dma((2,)),
            dma((2,)),
            dma((4,)),
            dma((4,)),
            dma((6,)),
        ],
        compiler_params=pltpu.CompilerParams(
            collective_id=0, has_side_effects=True, vmem_limit_bytes=60 << 20
        ),
    )(
        down_inputs[0, 0].T,
        up_inputs[0, 0].T,
        down_cot[0, 0].T,
        up_cot[0, 0].T,
        segment_ids,
        patch_rows,
        patch_cols,
        w_qkv.reshape(ROWS, D),
        w_out[0],
    )
    outs = pl.pallas_call(
        place,
        out_shape=shapes,
        in_specs=[hbm] * 4,
        out_specs=(hbm,) * 4,
        scratch_shapes=[pltpu.VMEM(x.shape, BF16) for x in shapes] + [dma((2, 10))],
        compiler_params=pltpu.CompilerParams(vmem_limit_bytes=60 << 20),
    )(*outs)
    return (
        outs[0].T[None, None],
        outs[1].T[None, None],
        outs[2].reshape(w_qkv.shape),
        outs[3][None],
    )


def solution(mesh):
    return jax.shard_map(
        per_device,
        mesh=mesh,
        in_specs=(
            P("dp", "phase", None, "tp"),
            P("dp", "phase", None, "tp"),
            P("dp", "phase", None, "tp"),
            P("dp", "phase", None, "tp"),
            P(None, "dp", None, None),
            P(None, "dp", None, None),
            P(None, "dp", None, None),
            P("phase", None, "tp", None),
            P("phase", "tp", None),
        ),
        out_specs=(
            P("dp", "phase", None, "tp"),
            P("dp", "phase", None, "tp"),
            P("phase", None, "tp", None),
            P("phase", "tp", None),
        ),
        check_vma=False,
    )
```
